32 devices in a mesh: space: 16 (over z, y, core), coil: 2 (over x).
Axes of the slice: x: 2, y: 2, z: 4, core: 2. Of those that a mesh axis runs over, the one named last changes fastest.
Arguments:
- spatial_coef: bfloat16 [16, 128, 128, 2, 128], P('coil', 'space'), may hold values from -6 to 6
- temporal_basis: bfloat16 [2, 16, 4], replicated, may hold values from -1.5 to 1.5
- coil_maps: bfloat16 [8, 128, 128, 2, 128], P('coil', 'space'), may hold values from -6 to 6
- field_steps: int32 [128, 128, 128], P('space'), may hold values from 0 to 255
- kspace_data: bfloat16 [8, 4, 128, 128, 2, 128], P('coil', None, None, 'space'), may hold values from -6 to 6
- sample_mask: int32 [4, 128, 128], P(None, 'space'), may hold values 0 or 1
Outputs:
- gradient: float32 [16, 128, 128, 2, 128], P('coil', 'space')
The draws below stay inside these ranges and needn't reach their ends.
Inputs may be any that keep to these rules, and one draw needn't show every extreme that they name: `sample_mask`: 1 where a phase-encoding line is sampled at that point, else 0.
All inputs are finite; a program needn't handle non-finite values. No bound on the sum of `sample_mask` on one device may be relied on, other than what follows from the above.
Results may differ from the reference program's by a relative error of at most 0.014.
Values may be sent and summed in bfloat16 or wider, within the bound.
No kernel may reach another device: no remote copies, remote signals or barrier semaphores. Data moves between devices by JAX's collectives and lax.ppermute only.
A program may use at most 128 MiB of HBM per device.

```python
import math
import jax
import jax.numpy as jnp
from jax import lax

NX = 128
NY = 128
NZ = 128
RANK = 16
PTS = 4
STEPS_CYCLE = 256
COILS = 8


def set_ends(drawn, stream_key, smallest, top_value):
    longest = drawn.shape.index(max(drawn.shape))
    spots = []
    for shift in (0, 1):
        where = [jax.random.randint(jax.random.fold_in(stream_key, axis), (), 0, length) for axis, length in enumerate(drawn.shape)]
        where[longest] = (where[longest] + shift) % drawn.shape[longest]
        spots.append(tuple(where))
    return drawn.at[spots[0]].set(smallest).at[spots[1]].set(top_value)


def block_levels(stream_key, dims, split, smallest, high):
    gain, own = 1.0, jax.random.fold_in(stream_key, 6)
    for position, blocks in split:
        steps = jnp.exp(jax.random.uniform(jax.random.fold_in(own, position), (blocks,), jnp.float32, smallest / len(split), high / len(split)))
        gain = gain * jnp.repeat(steps, dims[position] // blocks).reshape([-1 if axis == position else 1 for axis in range(len(dims))])
    return gain


def bell_draw(key, dims, deviation, limit, pieces=(), kind=jnp.bfloat16):
    factor_of = block_levels(key, dims, pieces, -0.22, 0.18) if pieces else 1.0
    result = jax.random.normal(key, dims, jnp.float32) * deviation * factor_of
    return jnp.minimum(jnp.maximum(result, -limit), limit).astype(kind)


def setup_inputs(seed: int = 0) -> dict:
    key_of = jax.random.split(jax.random.key(seed), 7)
    spatial_coef = bell_draw(key_of[0], (RANK, NX, NY, 2, NZ), 1.0, 6.0, ((0, 2), (1, 16)))
    temporal_basis = bell_draw(key_of[1], (2, RANK, PTS), RANK ** -0.5, 1.5)
    coil_maps = bell_draw(key_of[2], (COILS, NX, NY, 2, NZ), 0.5, 6.0, ((0, 2), (1, 16)))
    field_steps = set_ends(jax.random.randint(key_of[3], (NX, NY, NZ), 0, STEPS_CYCLE), jax.random.fold_in(key_of[3], 1), 0, STEPS_CYCLE - 1).astype(jnp.int32)
    kspace_data = bell_draw(key_of[4], (COILS, PTS, NX, NY, 2, NZ), 0.5, 6.0, ((0, 2), (3, 16)))
    sample_mask = set_ends((jax.random.randint(key_of[5], (PTS, NY, NZ), 0, 2) < 1).astype(jnp.int32), jax.random.fold_in(key_of[5], 1), 0, 1)
    return {"spatial_coef": spatial_coef, "temporal_basis": temporal_basis, "coil_maps": coil_maps, "field_steps": field_steps, "kspace_data": kspace_data, "sample_mask": sample_mask}


def dft_table(length, sign):
    index = jnp.arange(length, dtype=jnp.int32)
    steps = index[:, None] * index[None, :] % length
    angle = steps.astype(jnp.float32) * (2.0 * math.pi / length)
    scale = 1.0 / math.sqrt(length)
    cosine = jnp.cos(angle) * scale
    sine = jnp.sin(angle) * (sign * scale)
    upper = jnp.stack([cosine, sine], axis=1)
    lower = jnp.stack([-sine, cosine], axis=1)
    return jnp.stack([upper, lower], axis=0).astype(jnp.bfloat16)

def forward_mix(basis):
    real_part = basis[0]
    imaginary = basis[1]
    return jnp.stack([jnp.stack([real_part, imaginary], -1), jnp.stack([-imaginary, real_part], -1)], 1)

def adjoint_mix(basis):
    real_part = basis[0].T
    imaginary = basis[1].T
    return jnp.stack([jnp.stack([real_part, -imaginary], -1), jnp.stack([imaginary, real_part], -1)], 1)

def phase_parts(field_steps, points):
    counter = jnp.arange(1, points + 1, dtype=jnp.int32)
    steps = field_steps[None] * counter[:, None, None, None] % STEPS_CYCLE
    angle = steps.astype(jnp.float32) * (2.0 * math.pi / STEPS_CYCLE)
    return (jnp.cos(angle), jnp.sin(angle))

def transform(volume, table, form):
    return jnp.einsum(form, volume.astype(jnp.float32), table.astype(jnp.float32), precision=lax.Precision.HIGHEST)

def reference(spatial_coef, temporal_basis, coil_maps, field_steps, kspace_data, sample_mask):
    points = temporal_basis.shape[2]
    basis = temporal_basis.astype(jnp.float32)
    image = jnp.einsum('lxypz,lptq->txyqz', spatial_coef.astype(jnp.float32), forward_mix(basis), precision=lax.Precision.HIGHEST)
    cosine, sine = phase_parts(field_steps, points)
    image_real = image[:, :, :, 0]
    image_imaginary = image[:, :, :, 1]
    turned_real = cosine * image_real - sine * image_imaginary
    turned_imaginary = sine * image_real + cosine * image_imaginary
    depth_fwd = dft_table(NZ, -1.0)
    rows_fwd = dft_table(NY, -1.0)
    first_fwd = dft_table(NX, -1.0)
    depth_inv = dft_table(NZ, 1.0)
    rows_inv = dft_table(NY, 1.0)
    first_inv = dft_table(NX, 1.0)
    mask_float = sample_mask.astype(jnp.float32)[:, None, :, None, :]

    def per_coil(carry, items):
        maps, data = items
        map_real = maps[:, :, 0].astype(jnp.float32)
        map_imaginary = maps[:, :, 1].astype(jnp.float32)
        coil_real = map_real * turned_real - map_imaginary * turned_imaginary
        coil_imaginary = map_real * turned_imaginary + map_imaginary * turned_real
        coil_image = jnp.stack([coil_real, coil_imaginary], axis=3).astype(jnp.bfloat16)
        depth_pass = transform(coil_image, depth_fwd, 'txypz,pzqk->txyqk').astype(jnp.bfloat16)
        row_pass = transform(depth_pass, rows_fwd, 'txypz,pyqk->txkqz').astype(jnp.bfloat16)
        kspace = transform(row_pass, first_fwd, 'txypz,pxqk->tkyqz')
        residual = (mask_float * (kspace - data.astype(jnp.float32))).astype(jnp.bfloat16)
        back_first = transform(residual, first_inv, 'txypz,pxqk->tkyqz').astype(jnp.bfloat16)
        back_rows = transform(back_first, rows_inv, 'txypz,pyqk->txkqz').astype(jnp.bfloat16)
        back_image = transform(back_rows, depth_inv, 'txypz,pzqk->txyqk')
        back_real = back_image[:, :, :, 0]
        back_imaginary = back_image[:, :, :, 1]
        sum_real = carry[0] + (map_real * back_real + map_imaginary * back_imaginary)
        sum_imaginary = carry[1] + (map_real * back_imaginary - map_imaginary * back_real)
        return ((sum_real, sum_imaginary), None)
    zeros = jnp.zeros(turned_real.shape, jnp.float32)
    (sum_real, sum_imaginary), unused = lax.scan(per_coil, (zeros, zeros), (coil_maps, kspace_data))
    combined_real = cosine * sum_real + sine * sum_imaginary
    combined_imaginary = cosine * sum_imaginary - sine * sum_real
    combined = jnp.stack([combined_real, combined_imaginary], axis=3)
    return jnp.einsum('txypz,tplq->lxyqz', combined, adjoint_mix(basis), precision=lax.Precision.HIGHEST)
```

```python
import math

import jax
import jax.numpy as jnp
from jax import lax
from jax.sharding import PartitionSpec as P

STEPS_CYCLE = 256


def dft_table(length, sign):
    index = jnp.arange(length, dtype=jnp.int32)
    steps = index[:, None] * index[None, :] % length
    angle = steps.astype(jnp.float32) * (2.0 * math.pi / length)
    scale = 1.0 / math.sqrt(length)
    cosine = jnp.cos(angle) * scale
    sine = jnp.sin(angle) * (sign * scale)
    upper = jnp.stack([cosine, sine], axis=1)
    lower = jnp.stack([-sine, cosine], axis=1)
    return jnp.stack([upper, lower], axis=0).astype(jnp.bfloat16)


def forward_mix(basis):
    real_part = basis[0]
    imaginary = basis[1]
    return jnp.stack(
        [jnp.stack([real_part, imaginary], -1), jnp.stack([-imaginary, real_part], -1)], 1
    )


def adjoint_mix(basis):
    real_part = basis[0].T
    imaginary = basis[1].T
    return jnp.stack(
        [jnp.stack([real_part, -imaginary], -1), jnp.stack([imaginary, real_part], -1)], 1
    )


def phase_parts(field_steps, points):
    counter = jnp.arange(1, points + 1, dtype=jnp.int32)
    steps = field_steps[None] * counter[:, None, None, None] % STEPS_CYCLE
    angle = steps.astype(jnp.float32) * (2.0 * math.pi / STEPS_CYCLE)
    return (jnp.cos(angle), jnp.sin(angle))


def transform(volume, table, form):
    return jnp.einsum(form, volume, table, preferred_element_type=jnp.float32)


def over_groups(part, axis):
    groups = lax.axis_size(axis)
    sent = part.astype(jnp.bfloat16)
    total = part
    for shift in range(1, groups):
        pairs = [(g, (g + shift) % groups) for g in range(groups)]
        total = total + lax.ppermute(sent, axis, pairs).astype(jnp.float32)
    return total


def shards(spatial_coef, temporal_basis, coil_maps, field_steps, kspace_data, sample_mask):
    points = temporal_basis.shape[2]
    ranks = spatial_coef.shape[0]
    basis = lax.dynamic_slice_in_dim(
        temporal_basis, lax.axis_index("coil") * ranks, ranks, axis=1
    )
    first_count = kspace_data.shape[2]
    row_count = coil_maps.shape[2]
    depth_count = coil_maps.shape[4]
    mask_here = sample_mask.astype(jnp.bfloat16)
    mask_all = lax.all_gather(mask_here, "space", axis=1, tiled=True)
    arrived = []
    for t in range(points):
        measured = kspace_data[:, t] * mask_here[t][None, None, :, None, :]
        local = transform(measured, dft_table(first_count, 1.0), "cxypz,pxqk->ckyqz").astype(
            jnp.bfloat16
        )
        arrived.append(lax.all_to_all(local, "space", split_axis=1, concat_axis=2, tiled=True))
    cosine, sine = phase_parts(field_steps, points)
    map_real = coil_maps[:, :, :, 0].astype(jnp.float32)
    map_imaginary = coil_maps[:, :, :, 1].astype(jnp.float32)
    mixed = forward_mix(basis)
    combined = []
    for t in range(points):
        image = over_groups(
            jnp.einsum(
                "lxypz,lpq->xyqz",
                spatial_coef,
                mixed[:, :, t],
                preferred_element_type=jnp.float32,
            ),
            "coil",
        )
        turned_real = cosine[t] * image[:, :, 0] - sine[t] * image[:, :, 1]
        turned_imaginary = sine[t] * image[:, :, 0] + cosine[t] * image[:, :, 1]
        coil_real = map_real * turned_real - map_imaginary * turned_imaginary
        coil_imaginary = map_real * turned_imaginary + map_imaginary * turned_real
        coil_image = jnp.stack([coil_real, coil_imaginary], axis=3).astype(jnp.bfloat16)
        depth_pass = transform(coil_image, dft_table(depth_count, -1.0), "cxypz,pzqk->cxyqk")
        row_pass = transform(
            depth_pass.astype(jnp.bfloat16), dft_table(row_count, -1.0), "cxypz,pyqk->cxkqz"
        )
        mask_float = mask_all[t].astype(jnp.float32)[None, None, :, None, :]
        back_first = (mask_float * row_pass - arrived[t].astype(jnp.float32)).astype(jnp.bfloat16)
        back_rows = transform(back_first, dft_table(row_count, 1.0), "cxypz,pyqk->cxkqz")
        back_image = transform(
            back_rows.astype(jnp.bfloat16), dft_table(depth_count, 1.0), "cxypz,pzqk->cxyqk"
        )
        back_real = back_image[:, :, :, 0]
        back_imaginary = back_image[:, :, :, 1]
        sum_real = jnp.sum(map_real * back_real + map_imaginary * back_imaginary, axis=0)
        sum_imaginary = jnp.sum(map_real * back_imaginary - map_imaginary * back_real, axis=0)
        combined_real = cosine[t] * sum_real + sine[t] * sum_imaginary
        combined_imaginary = cosine[t] * sum_imaginary - sine[t] * sum_real
        combined.append(
            over_groups(jnp.stack([combined_real, combined_imaginary], axis=2), "coil")
        )
    return jnp.einsum(
        "txypz,tplq->lxyqz",
        jnp.stack(combined),
        adjoint_mix(basis.astype(jnp.float32)),
        precision=lax.Precision.HIGHEST,
    )


def solution(mesh):
    in_specs = (
        P("coil", "space", None, None, None),
        P(),
        P("coil", "space", None, None, None),
        P("space", None, None),
        P("coil", None, None, "space", None, None),
        P(None, "space", None),
    )
    out_specs = P("coil", "space", None, None, None)
    return jax.shard_map(shards, mesh=mesh, in_specs=in_specs, out_specs=out_specs, check_vma=False)
```

```python
import functools
import math

import jax
import jax.numpy as jnp
import ml_dtypes
import numpy as np
from jax import lax
from jax.experimental import pallas as pl
from jax.experimental.pallas import tpu as pltpu
from jax.sharding import PartitionSpec as P

STEPS_CYCLE = 256
SENT_EIGHTHS = 5
PLANES = 4
SOURCES = 4
DATA_COILS = 2
VMEM_BYTES = 24 * 2**20
F32 = jnp.float32
BF16 = jnp.bfloat16


def real_table(length, sign, out_interleaved=False):
    index = np.arange(length)
    angle = (index[:, None] * index[None, :] % length) * (2.0 * math.pi / length)
    cosine = np.cos(angle) / math.sqrt(length)
    sine = sign * np.sin(angle) / math.sqrt(length)
    table = np.block([[cosine, -sine], [sine, cosine]])
    if out_interleaved:
        table = table.reshape(2, length, 2 * length).swapaxes(0, 1).reshape(2 * length, 2 * length)
    return jnp.asarray(table.astype(np.float32).astype(ml_dtypes.bfloat16))


def params():
    return pltpu.CompilerParams(vmem_limit_bytes=VMEM_BYTES)


def cost(flops, moved):
    return pl.CostEstimate(flops=int(flops), bytes_accessed=int(moved), transcendentals=0)


def whole_block(shape):
    return pl.BlockSpec(shape, lambda *_: (0,) * len(shape))


def unit_turn(steps):
    x = ((steps & (STEPS_CYCLE - 1)) - STEPS_CYCLE // 2).astype(F32) * (2.0 * math.pi / STEPS_CYCLE)
    square = x * x
    cosine = jnp.zeros_like(x)
    sine = jnp.zeros_like(x)
    for k in range(9, -1, -1):
        cosine = cosine * square + (-1.0) ** k / math.factorial(2 * k)
        sine = sine * square + (-1.0) ** k / math.factorial(2 * k + 1)
    return -cosine, -sine * x


def mix_factors(basis, block, interleaved):
    real, imaginary = basis[0], basis[1]
    eye = jnp.eye(block, dtype=basis.dtype)
    forward = jnp.stack([jnp.stack([real, -imaginary]), jnp.stack([imaginary, real])])
    adjoint = jnp.stack([jnp.stack([real, imaginary]), jnp.stack([-imaginary, real])])
    ranks, points = real.shape
    if interleaved:
        return jnp.einsum("qplt,yz->lyqtpz", adjoint, eye).reshape(
            ranks * block * 2, points * 2 * block
        )
    return jnp.einsum("qplt,yz->tqylzp", forward, eye).reshape(
        points * 2 * block, ranks * block * 2
    )


def image_kernel(points, block, mix_ref, order_ref, coef_ref, steps_ref, maps_ref, *rest):
    turned_refs, phase_refs = rest[:points], rest[points : 2 * points]
    planes_ref, mixed = rest[2 * points :]
    ranks, planes, rows2, depth = coef_ref.shape
    coils = maps_ref.shape[0]
    rows = rows2 // 2
    blocks = rows // block
    for x in range(planes):
        pair = 2 if blocks % 2 == 0 else 1
        for i in range(0, blocks, pair):
            columns = [
                jnp.concatenate(
                    [coef_ref[l, x, 2 * block * k : 2 * block * (k + 1), :] for l in range(ranks)],
                    axis=0,
                )
                for k in range(i, i + pair)
            ]
            image = jnp.dot(
                mix_ref[...], jnp.concatenate(columns, axis=1), preferred_element_type=F32
            )
            for k in range(pair):
                for j in range(2 * points):
                    mixed[x % 2, j, (i + k) * block : (i + k + 1) * block, :] = image[
                        j * block : (j + 1) * block, k * depth : (k + 1) * depth
                    ]
        cosine, sine = unit_turn(steps_ref[x])
        now_cosine, now_sine = cosine, sine
        for t in range(points):
            if t:
                now_cosine, now_sine = (
                    now_cosine * cosine - now_sine * sine,
                    now_sine * cosine + now_cosine * sine,
                )
            real, imaginary = mixed[x % 2, 2 * t], mixed[x % 2, 2 * t + 1]
            turned_refs[t][x, 0] = (now_cosine * real - now_sine * imaginary).astype(BF16)
            turned_refs[t][x, 1] = (now_sine * real + now_cosine * imaginary).astype(BF16)
            phase_refs[t][x, 0] = now_cosine
            phase_refs[t][x, 1] = now_sine
        pair = 2 if coils % 2 == 0 else 1
        for c in range(0, coils, pair):
            both = jnp.concatenate([maps_ref[c + k, x] for k in range(pair)], axis=1)
            parted = jnp.dot(order_ref[...], both, preferred_element_type=F32).astype(BF16)
            for k in range(pair):
                planes_ref[c + k, x] = parted[:, k * depth : (k + 1) * depth].reshape(
                    2, rows, depth
                )


def make_images(mix, coef, steps, maps, points):
    ranks, slab, rows, depth = coef.shape
    coils = maps.shape[0]
    step = math.gcd(slab, PLANES)
    plane = (2, rows // 2, depth)
    plane_block = pl.BlockSpec((step,) + plane, lambda x: (x, 0, 0, 0))
    order = np.eye(rows, dtype=np.float32).reshape(rows // 2, 2, rows).swapaxes(0, 1)
    order = jnp.asarray(order.reshape(rows, rows).astype(ml_dtypes.bfloat16))
    outs = pl.pallas_call(
        functools.partial(image_kernel, points, mix.shape[0] // (2 * points)),
        grid=(slab // step,),
        in_specs=[
            whole_block(mix.shape),
            whole_block(order.shape),
            pl.BlockSpec((ranks, step, rows, depth), lambda x: (0, x, 0, 0)),
            pl.BlockSpec((step, rows // 2, depth), lambda x: (x, 0, 0)),
            pl.BlockSpec((coils, step, rows, depth), lambda x: (0, x, 0, 0)),
        ],
        out_specs=[plane_block] * (2 * points)
        + [pl.BlockSpec((coils, step) + plane, lambda x: (0, x, 0, 0, 0))],
        out_shape=[jax.ShapeDtypeStruct((slab,) + plane, BF16)] * points
        + [jax.ShapeDtypeStruct((slab,) + plane, F32)] * points
        + [jax.ShapeDtypeStruct((coils, slab) + plane, BF16)],
        scratch_shapes=[pltpu.VMEM((2, 2 * points, rows // 2, depth), F32)],
        compiler_params=params(),
        cost_estimate=cost(4e9, 16e6),
        name="images",
    )(mix, order, coef, steps, maps)
    return outs[:points], outs[points : 2 * points], outs[2 * points]


def rank_kernel(slots, mask_ref, place_ref, plane_ref, base_ref):
    sources, points, slab_rows, depth = mask_ref.shape
    rows = sources * slab_rows
    before = lax.broadcasted_iota(jnp.int32, (depth, depth), 0) < lax.broadcasted_iota(
        jnp.int32, (depth, depth), 1
    )
    above = lax.broadcasted_iota(jnp.int32, (rows, rows), 0)
    left = lax.broadcasted_iota(jnp.int32, (rows, rows), 1)
    same = left // slab_rows == above // slab_rows
    lower = ((left < above) & same).astype(BF16)
    upper = ((above < left) & same).astype(BF16)
    for t in range(points):
        mask = mask_ref[:, t].astype(F32).reshape(rows, depth)
        packed = mask.astype(BF16)
        within = jnp.dot(packed, before.astype(BF16), preferred_element_type=F32)
        totals = jnp.dot(packed, jnp.ones((depth, depth), BF16), preferred_element_type=F32)
        starts = jnp.dot(lower, totals.astype(BF16), preferred_element_type=F32)
        rank = within + starts
        place = rank - jnp.floor(rank * (1.0 / depth)) * depth
        place_ref[t] = jnp.where((mask > 0.0) & (rank < slots), place, -1.0)
        plane_ref[t] = packed
        across = lax.dot_general(
            jnp.ones((8, depth), BF16), packed, (((1,), (1,)), ((), ())), preferred_element_type=F32
        )
        base_ref[t] = jnp.dot(across.astype(BF16), upper, preferred_element_type=F32).astype(
            jnp.int32
        )


def rank_cells(mask_all, slots):
    sources, points, slab_rows, depth = mask_all.shape
    rows = sources * slab_rows
    return pl.pallas_call(
        functools.partial(rank_kernel, slots),
        out_shape=[
            jax.ShapeDtypeStruct((points, rows, depth), F32),
            jax.ShapeDtypeStruct((points, rows, depth), BF16),
            jax.ShapeDtypeStruct((points, 8, rows), jnp.int32),
        ],
        compiler_params=params(),
        cost_estimate=cost(1e8, 1e6),
        name="ranks",
    )(mask_all)


def data_kernel(tiles, extra, table_ref, mask_ref, extra_ref, data_ref, out_ref, chosen):
    slab_rows, depth = mask_ref.shape[1:]
    dests, _, held, width, _ = out_ref.shape

    @pl.when(pl.program_id(1) == 0)
    def choose():
        mask = mask_ref[0]
        before = lax.broadcasted_iota(jnp.int32, (depth, depth), 0) < lax.broadcasted_iota(
            jnp.int32, (depth, depth), 1
        )
        within = jnp.dot(mask, before.astype(BF16), preferred_element_type=F32)
        totals = jnp.dot(mask, jnp.ones((depth, depth), BF16), preferred_element_type=F32)
        slot = lax.broadcasted_iota(jnp.int32, (tiles * depth, depth), 0).astype(F32)
        start = jnp.zeros((1, depth), F32)
        wide = mask.astype(F32)
        for k in range(slab_rows):
            rank = jnp.where(wide[k : k + 1] > 0.0, within[k : k + 1] + start, -1.0)
            chosen[:, k * depth : (k + 1) * depth] = jnp.where(slot == rank, 1.0, 0.0).astype(BF16)
            start = start + totals[k : k + 1]
        for e in range(extra):
            out_ref[:, 0, held - extra + e] = jnp.broadcast_to(
                extra_ref[e][None], (dests, width, depth)
            )

    for c in range(data_ref.shape[0]):
        data = jnp.swapaxes(data_ref[c, 0], 0, 1)
        cells = jnp.concatenate(
            [jnp.concatenate([data[2 * k], data[2 * k + 1]], axis=0) for k in range(slab_rows)],
            axis=1,
        )
        kept = lax.dot_general(
            cells, chosen[...], (((1,), (1,)), ((), ())), preferred_element_type=F32
        ).astype(BF16)
        turned = jnp.dot(table_ref[...], kept, preferred_element_type=F32)
        for a in range(tiles):
            part = turned[:, a * depth : (a + 1) * depth].reshape(dests, width, depth)
            at = (pl.program_id(1) * data_ref.shape[0] + c) * tiles + a
            out_ref[:, 0, at] = part.astype(BF16)


def transform_data(table, mask, extra, data, start, count, dests, tiles):
    coils, points, first, rows2, depth = data.shape
    width = 2 * first // dests
    step = math.gcd(coils, DATA_COILS)
    more = 0 if start else extra.shape[0]
    held = coils * tiles + more
    return pl.pallas_call(
        functools.partial(data_kernel, tiles, more),
        grid=(count, coils // step),
        in_specs=[
            whole_block(table.shape),
            pl.BlockSpec((1, rows2 // 2, depth), lambda t, c: (start + t, 0, 0)),
            whole_block(extra.shape),
            pl.BlockSpec((step, 1, first, rows2, depth), lambda t, c: (c, start + t, 0, 0, 0)),
        ],
        out_specs=pl.BlockSpec((dests, 1, held, width, depth), lambda t, c: (0, t, 0, 0, 0)),
        out_shape=jax.ShapeDtypeStruct((dests, count, held, width, depth), BF16),
        scratch_shapes=[pltpu.VMEM((tiles * depth, rows2 // 2 * depth), BF16)],
        compiler_params=pltpu.CompilerParams(vmem_limit_bytes=56 * 2**20),
        cost_estimate=cost(2e9 * count, 8e6 * count),
        name="data",
    )(table, mask, extra, data)


def forward_kernel(depth_ref, row_ref, own_ref, far_ref, maps_ref, out_ref):
    coils, planes, _, rows, depth = maps_ref.shape
    pair = 2 if coils % 2 == 0 else 1
    for x in range(planes):
        real = own_ref[x, 0].astype(F32) + far_ref[x, 0].astype(F32)
        imaginary = own_ref[x, 1].astype(F32) + far_ref[x, 1].astype(F32)
        for c in range(0, coils, pair):
            stacked = []
            for k in range(c, c + pair):
                map_real = maps_ref[k, x, 0].astype(F32)
                map_imaginary = maps_ref[k, x, 1].astype(F32)
                coil_real = (map_real * real - map_imaginary * imaginary).astype(BF16)
                coil_imaginary = (map_real * imaginary + map_imaginary * real).astype(BF16)
                stacked.append(jnp.concatenate([coil_real, coil_imaginary], axis=1))
            deep = jnp.dot(
                jnp.concatenate(stacked, axis=0), depth_ref[...], preferred_element_type=F32
            ).astype(BF16)
            columns = [
                jnp.concatenate(
                    [
                        deep[k * rows : (k + 1) * rows, :depth],
                        deep[k * rows : (k + 1) * rows, depth:],
                    ],
                    axis=0,
                )
                for k in range(pair)
            ]
            lines = jnp.dot(
                row_ref[...], jnp.concatenate(columns, axis=1), preferred_element_type=F32
            )
            for k in range(pair):
                out_ref[c + k, x] = lines[:, k * depth : (k + 1) * depth].astype(BF16)


def forward_lines(depth_table, row_table, own, far, maps):
    coils, slab, _, rows, depth = maps.shape
    step = math.gcd(slab, PLANES)
    plane_block = pl.BlockSpec((step, 2, rows, depth), lambda x: (x, 0, 0, 0))
    return pl.pallas_call(
        forward_kernel,
        grid=(slab // step,),
        in_specs=[
            whole_block(depth_table.shape),
            whole_block(row_table.shape),
            plane_block,
            plane_block,
            pl.BlockSpec((coils, step, 2, rows, depth), lambda x: (0, x, 0, 0, 0)),
        ],
        out_specs=pl.BlockSpec((coils, step, 2 * rows, depth), lambda x: (0, x, 0, 0)),
        out_shape=jax.ShapeDtypeStruct((coils, slab, 2 * rows, depth), BF16),
        compiler_params=params(),
        cost_estimate=cost(3e9, 8e6),
        name="forward",
    )(depth_table, row_table, own, far, maps)


def back_kernel(
    spreads, tiles, depth_ref, row_ref, base_ref, place_ref, mask_ref, data_ref, lines_ref,
    maps_ref, phase_ref, out_ref, held
):
    coils, planes = maps_ref.shape[:2]
    rows, depth = maps_ref.shape[3:]
    sources, _, _, width, _ = data_ref.shape
    high = coils * width
    step = pl.program_id(0)
    slab_rows = rows // (spreads * sources)

    @pl.when(step < spreads)
    def spread():
        lane = lax.broadcasted_iota(jnp.int32, (high, depth), 1)
        slot = lax.broadcasted_iota(jnp.int32, (depth, depth), 0).astype(F32)
        for s in range(sources):
            first = pl.multiple_of((step * sources + s) * slab_rows, slab_rows)
            sides = []
            for k in range(slab_rows):
                base = base_ref[first + k]
                at = jnp.minimum(base // depth, tiles - 1)
                after = jnp.minimum(at + 1, tiles - 1)
                low, top = (
                    jnp.concatenate(
                        [data_ref[s, 0, c * tiles + i].astype(F32) for c in range(coils)], axis=0
                    )
                    for i in (at, after)
                )
                sides.append(jnp.where(lane >= base % depth, low, top).astype(BF16))
            places = place_ref[0, pl.ds(first, slab_rows), :]
            spread_out = [
                jnp.dot(
                    sides[k],
                    jnp.where(slot == places[k : k + 1], 1.0, 0.0).astype(BF16),
                    preferred_element_type=F32,
                )
                for k in range(slab_rows)
            ]
            span = slab_rows * high
            held[pl.ds(pl.multiple_of(first * high, span), span), :] = jnp.concatenate(
                spread_out, axis=0
            )

    @pl.when(step >= spreads)
    def back():
        pair = 2 if coils % 2 == 0 else 1
        mask = mask_ref[0].astype(F32)
        mask = jnp.concatenate([mask, mask], axis=0)
        for j in range(planes):
            x = (step - spreads) * planes + j
            sum_real = sum_imaginary = None
            for c in range(0, coils, pair):
                columns = []
                for k in range(c, c + pair):
                    parts = [
                        held[pl.ds(k * width + 2 * x + p, rows, stride=high), :] for p in range(2)
                    ]
                    columns.append(
                        (lines_ref[k, j].astype(F32) * mask - jnp.concatenate(parts, axis=0)).astype(BF16)
                    )
                turned = jnp.dot(
                    row_ref[...], jnp.concatenate(columns, axis=1), preferred_element_type=F32
                ).astype(BF16)
                stacked = []
                for k in range(pair):
                    part = turned[:, k * depth : (k + 1) * depth]
                    stacked.append(jnp.concatenate([part[:rows], part[rows:]], axis=1))
                images = jnp.dot(
                    jnp.concatenate(stacked, axis=0), depth_ref[...], preferred_element_type=F32
                )
                for k in range(pair):
                    map_real = maps_ref[c + k, j, 0].astype(F32)
                    map_imaginary = maps_ref[c + k, j, 1].astype(F32)
                    back_real = images[k * rows : (k + 1) * rows, :depth]
                    back_imaginary = images[k * rows : (k + 1) * rows, depth:]
                    term_real = map_real * back_real + map_imaginary * back_imaginary
                    term_imaginary = map_real * back_imaginary - map_imaginary * back_real
                    sum_real = term_real if sum_real is None else sum_real + term_real
                    sum_imaginary = (
                        term_imaginary if sum_imaginary is None else sum_imaginary + term_imaginary
                    )
            cosine, sine = phase_ref[j, 0], phase_ref[j, 1]
            out_ref[j, 0] = (cosine * sum_real + sine * sum_imaginary).astype(BF16)
            out_ref[j, 1] = (cosine * sum_imaginary - sine * sum_real).astype(BF16)


def back_images(depth_table, row_table, ranks, data, lines, maps, phase, t, part, tiles):
    coils, slab, _, rows, depth = maps.shape
    place, mask, base = ranks
    sources, _, held, width, _ = data.shape
    step = math.gcd(slab, PLANES)
    some = math.gcd(sources, SOURCES)
    spreads = sources // some

    def plane(i):
        return jnp.maximum(i - spreads, 0)

    plane_block = pl.BlockSpec((step, 2, rows, depth), lambda i: (plane(i), 0, 0, 0))
    return pl.pallas_call(
        functools.partial(back_kernel, spreads, tiles),
        grid=(spreads + slab // step,),
        in_specs=[
            whole_block(depth_table.shape),
            whole_block(row_table.shape),
            pl.BlockSpec(memory_space=pltpu.SMEM),
            pl.BlockSpec((1, rows, depth), lambda i: (t, 0, 0)),
            pl.BlockSpec((1, rows, depth), lambda i: (t, 0, 0)),
            pl.BlockSpec(
                (some, 1, held, width, depth),
                lambda i: (jnp.minimum(i, spreads - 1), part, 0, 0, 0),
            ),
            pl.BlockSpec((coils, step, 2 * rows, depth), lambda i: (0, plane(i), 0, 0)),
            pl.BlockSpec((coils, step, 2, rows, depth), lambda i: (0, plane(i), 0, 0, 0)),
            plane_block,
        ],
        out_specs=plane_block,
        out_shape=jax.ShapeDtypeStruct((slab, 2, rows, depth), BF16),
        scratch_shapes=[pltpu.VMEM((rows * coils * width, depth), F32)],
        compiler_params=params(),
        cost_estimate=cost(3e9, 10e6),
        name="back",
    )(depth_table, row_table, base[t, 0], place, mask, data, lines, maps, phase)


def gradient_kernel(points, block, mix_ref, *rest):
    own_refs, far_refs, out_ref = rest[:points], rest[points : 2 * points], rest[2 * points]
    ranks, planes, rows2, depth = out_ref.shape
    for x in range(planes):
        for i in range(rows2 // (2 * block)):
            at = slice(i * block, (i + 1) * block)
            columns = [
                jnp.concatenate(
                    [refs[t][x, p, at, :] for t in range(points) for p in range(2)], axis=0
                )
                for refs in (own_refs, far_refs)
            ]
            both = jnp.dot(
                mix_ref[...], jnp.concatenate(columns, axis=1), preferred_element_type=F32
            )
            total = both[:, :depth] + both[:, depth:]
            out_ref[:, x, 2 * i * block : 2 * (i + 1) * block, :] = total.reshape(
                ranks, 2 * block, depth
            )


def gradient(mix, own, far, ranks):
    points = len(own)
    slab, _, rows, depth = own[0].shape
    step = math.gcd(slab, 2)
    plane_block = pl.BlockSpec((step, 2, rows, depth), lambda x: (x, 0, 0, 0))
    return pl.pallas_call(
        functools.partial(gradient_kernel, points, mix.shape[1] // (2 * points)),
        grid=(slab // step,),
        in_specs=[whole_block(mix.shape)] + [plane_block] * (2 * points),
        out_specs=pl.BlockSpec((ranks, step, 2 * rows, depth), lambda x: (0, x, 0, 0)),
        out_shape=jax.ShapeDtypeStruct((ranks, slab, 2 * rows, depth), F32),
        compiler_params=params(),
        cost_estimate=cost(4e9, 12e6),
        name="gradient",
    )(mix, *own, *far)


def from_other_groups(part, axis):
    groups = lax.axis_size(axis)
    moved = [
        lax.ppermute(part, axis, [(g, (g + shift) % groups) for g in range(groups)])
        for shift in range(1, groups)
    ]
    if groups == 1:
        return jnp.zeros_like(part)
    if groups == 2:
        return moved[0]
    return sum(m.astype(F32) for m in moved).astype(BF16)


def shards(spatial_coef, temporal_basis, coil_maps, field_steps, kspace_data, sample_mask):
    points = temporal_basis.shape[2]
    ranks, slab, rows, _, depth = spatial_coef.shape
    coils = coil_maps.shape[0]
    first, slab_rows = kspace_data.shape[2:4]
    dests = lax.axis_size("space")
    basis = lax.dynamic_slice_in_dim(
        temporal_basis, lax.axis_index("coil") * ranks, ranks, axis=1
    )
    mix, adjoint = mix_factors(basis, 16, False), mix_factors(basis, 32, True)
    data = kspace_data.reshape(coils, points, first, 2 * slab_rows, depth)
    maps = coil_maps.reshape(coils, slab, 2 * rows, depth)
    coef = spatial_coef.reshape(ranks, slab, 2 * rows, depth)
    cells = slab_rows * depth
    tiles = -(-SENT_EIGHTHS * cells // (8 * depth))
    slots = tiles * depth
    width = 2 * first // dests
    mask_here = sample_mask.astype(BF16)
    held = -(-points * slab_rows // width)
    extra = jnp.pad(
        mask_here.reshape(points * slab_rows, depth),
        ((0, held * width - points * slab_rows), (0, 0)),
    ).reshape(held, width, depth)
    first_table = real_table(first, 1.0, out_interleaved=True)
    depth_forward, depth_back = real_table(depth, -1.0).T, real_table(depth, 1.0).T
    rows_forward, rows_back = real_table(rows, -1.0), real_table(rows, 1.0)

    def prepare(data, start, count):
        return transform_data(first_table, mask_here, extra, data, start, count, dests, tiles)

    def send(sent):
        return lax.all_to_all(sent, "space", split_axis=0, concat_axis=0, tiled=True)

    def back(t, ranked, here, lines):
        part = t - max(start for start, _ in spans if start <= t)
        own = back_images(
            depth_back, rows_back, ranked, here, lines, planes, phases[t], t, part, tiles
        )
        return own, from_other_groups(own, "coil")

    spans = [(0, 1), (1, points - 2), (points - 1, 1)] if points > 2 else [(0, points)]
    chunk_of = [i for i, (_, count) in enumerate(spans) for _ in range(count)]
    sent = [prepare(data, *spans[0])]
    arrived = [send(sent[0])]
    coef, _ = lax.optimization_barrier((coef, sent[0]))
    turned, phases, planes = make_images(mix, coef, field_steps, maps, points)
    others = [from_other_groups(part, "coil") for part in turned]
    lines = []
    for t in range(points):
        if t < len(spans) - 1:
            data, _ = lax.optimization_barrier((data, lines[-1] if lines else planes))
            sent.append(prepare(data, *spans[t + 1]))
            if t + 1 < len(spans) - 1:
                arrived.append(send(sent[-1]))
        lines.append(forward_lines(depth_forward, rows_forward, turned[t], others[t], planes))

    mask_all = arrived[0][:, 0, coils * tiles :].reshape(dests, held * width, depth)
    mask_all = mask_all[:, : points * slab_rows].reshape(dests, points, slab_rows, depth)
    ranked = rank_cells(mask_all, slots)
    early = [back(t, ranked, arrived[0], lines[t]) for t in range(points) if chunk_of[t] == 0]

    def finish(early, lines, arrived, last):
        arrived = arrived + [send(last)] if len(spans) > 1 else arrived
        done = list(early)
        for t in range(len(early), points):
            done.append(back(t, ranked, arrived[chunk_of[t]], lines[t]))
        own, far = zip(*done)
        return gradient(adjoint, own, far, ranks)

    def finish_more(early, lines, arrived, last):
        count = jnp.cumsum(mask_here.astype(F32).reshape(points, cells), axis=1)
        rest = jnp.where(count > slots, mask_here.reshape(points, cells), 0).astype(BF16)
        rest = rest.reshape(1, points, 1, slab_rows, 1, depth)
        table = real_table(first, 1.0).reshape(2, first, 2, first)
        moved = jnp.einsum(
            "ctxypz,qkpx->ctkqyz", kspace_data * rest, table, preferred_element_type=F32
        ).astype(BF16)
        moved = lax.all_to_all(moved, "space", split_axis=2, concat_axis=4, tiled=True)
        moved = moved.reshape(coils, points, slab, 2 * rows, depth)
        lines = [
            (lines[t].astype(F32) - moved[:, t].astype(F32)).astype(BF16) for t in range(points)
        ]
        early = [back(t, ranked, arrived[0], lines[t]) for t in range(len(early))]
        return finish(early, lines, arrived, last)

    most = jnp.max(jnp.sum(mask_all.astype(F32), axis=(2, 3)))
    result = lax.cond(most > slots, finish_more, finish, early, lines, arrived, sent[-1])
    return result.reshape(ranks, slab, rows, 2, depth)


def solution(mesh):
    in_specs = (
        P("coil", "space", None, None, None),
        P(),
        P("coil", "space", None, None, None),
        P("space", None, None),
        P("coil", None, None, "space", None, None),
        P(None, "space", None),
    )
    out_specs = P("coil", "space", None, None, None)
    return jax.shard_map(shards, mesh=mesh, in_specs=in_specs, out_specs=out_specs, check_vma=False)
```

```python
import functools
import math

import jax
import jax.numpy as jnp
import ml_dtypes
import numpy as np
from jax import lax
from jax.experimental import pallas as pl
from jax.experimental.pallas import tpu as pltpu
from jax.sharding import PartitionSpec as P

STEPS_CYCLE = 256
SENT_SIXTEENTHS = 9
PLANES = 4
BACK_PLANES = 8
SOURCES = 8
HEAD = 2
UNROLL = 2
GRADIENT_PLANES = 2
VMEM_BYTES = 24 * 2**20
F32 = jnp.float32
BF16 = jnp.bfloat16


def real_table(length, sign, out_interleaved=False):
    index = np.arange(length)
    angle = (index[:, None] * index[None, :] % length) * (2.0 * math.pi / length)
    cosine = np.cos(angle) / math.sqrt(length)
    sine = sign * np.sin(angle) / math.sqrt(length)
    table = np.block([[cosine, -sine], [sine, cosine]])
    if out_interleaved:
        table = table.reshape(2, length, 2 * length).swapaxes(0, 1).reshape(2 * length, 2 * length)
    return jnp.asarray(table.astype(np.float32).astype(ml_dtypes.bfloat16))


def params():
    return pltpu.CompilerParams(vmem_limit_bytes=VMEM_BYTES)


def cost(flops, moved):
    return pl.CostEstimate(flops=int(flops), bytes_accessed=int(moved), transcendentals=0)


def whole_block(shape):
    return pl.BlockSpec(shape, lambda *_: (0,) * len(shape))


def unit_turn(steps):
    x = ((steps & (STEPS_CYCLE - 1)) - STEPS_CYCLE // 2).astype(F32) * (2.0 * math.pi / STEPS_CYCLE)
    square = x * x
    cosine = jnp.zeros_like(x)
    sine = jnp.zeros_like(x)
    for k in range(9, -1, -1):
        cosine = cosine * square + (-1.0) ** k / math.factorial(2 * k)
        sine = sine * square + (-1.0) ** k / math.factorial(2 * k + 1)
    return -cosine, -sine * x


def mix_factors(basis, block, interleaved):
    real, imaginary = basis[0], basis[1]
    eye = jnp.eye(block, dtype=basis.dtype)
    forward = jnp.stack([jnp.stack([real, -imaginary]), jnp.stack([imaginary, real])])
    adjoint = jnp.stack([jnp.stack([real, imaginary]), jnp.stack([-imaginary, real])])
    ranks, points = real.shape
    if interleaved:
        return jnp.einsum("qplt,yz->lyqtpz", adjoint, eye).reshape(
            ranks * block * 2, points * 2 * block
        )
    return jnp.einsum("qplt,yz->tqylzp", forward, eye).reshape(
        points * 2 * block, ranks * block * 2
    )


def image_kernel(points, block, mix_ref, order_ref, coef_ref, steps_ref, maps_ref, *rest):
    turned_refs, phase_refs = rest[:points], rest[points : 2 * points]
    planes_ref, mixed = rest[2 * points :]
    ranks, planes, rows2, depth = coef_ref.shape
    coils = maps_ref.shape[0]
    rows = rows2 // 2
    blocks = rows // block
    @pl.loop(0, planes, unroll=math.gcd(planes, UNROLL))
    def one(x):
        pair = 2 if blocks % 2 == 0 else 1
        for i in range(0, blocks, pair):
            columns = [
                jnp.concatenate(
                    [coef_ref[l, x, 2 * block * k : 2 * block * (k + 1), :] for l in range(ranks)],
                    axis=0,
                )
                for k in range(i, i + pair)
            ]
            image = jnp.dot(
                mix_ref[...], jnp.concatenate(columns, axis=1), preferred_element_type=F32
            )
            for k in range(pair):
                for j in range(2 * points):
                    mixed[j, (i + k) * block : (i + k + 1) * block, :] = image[
                        j * block : (j + 1) * block, k * depth : (k + 1) * depth
                    ]
        cosine, sine = unit_turn(steps_ref[x])
        now_cosine, now_sine = cosine, sine
        for t in range(points):
            if t:
                now_cosine, now_sine = (
                    now_cosine * cosine - now_sine * sine,
                    now_sine * cosine + now_cosine * sine,
                )
            real, imaginary = mixed[2 * t], mixed[2 * t + 1]
            turned_refs[t][x, 0] = (now_cosine * real - now_sine * imaginary).astype(BF16)
            turned_refs[t][x, 1] = (now_sine * real + now_cosine * imaginary).astype(BF16)
            phase_refs[t][x, 0] = now_cosine
            phase_refs[t][x, 1] = now_sine
        pair = 2 if coils % 2 == 0 else 1
        for c in range(0, coils, pair):
            both = jnp.concatenate([maps_ref[c + k, x] for k in range(pair)], axis=1)
            parted = jnp.dot(order_ref[...], both, preferred_element_type=F32).astype(BF16)
            for k in range(pair):
                planes_ref[c + k, x] = parted[:, k * depth : (k + 1) * depth].reshape(
                    2, rows, depth
                )


def make_images(mix, coef, steps, maps, points):
    ranks, slab, rows, depth = coef.shape
    coils = maps.shape[0]
    step = math.gcd(slab, PLANES)
    plane = (2, rows // 2, depth)
    plane_block = pl.BlockSpec((step,) + plane, lambda x: (x, 0, 0, 0))
    order = np.eye(rows, dtype=np.float32).reshape(rows // 2, 2, rows).swapaxes(0, 1)
    order = jnp.asarray(order.reshape(rows, rows).astype(ml_dtypes.bfloat16))
    outs = pl.pallas_call(
        functools.partial(image_kernel, points, mix.shape[0] // (2 * points)),
        grid=(slab // step,),
        in_specs=[
            whole_block(mix.shape),
            whole_block(order.shape),
            pl.BlockSpec((ranks, step, rows, depth), lambda x: (0, x, 0, 0)),
            pl.BlockSpec((step, rows // 2, depth), lambda x: (x, 0, 0)),
            pl.BlockSpec((coils, step, rows, depth), lambda x: (0, x, 0, 0)),
        ],
        out_specs=[plane_block] * (2 * points)
        + [pl.BlockSpec((coils, step) + plane, lambda x: (0, x, 0, 0, 0))],
        out_shape=[jax.ShapeDtypeStruct((slab,) + plane, BF16)] * points
        + [jax.ShapeDtypeStruct((slab,) + plane, F32)] * points
        + [jax.ShapeDtypeStruct((coils, slab) + plane, BF16)],
        scratch_shapes=[pltpu.VMEM((2 * points, rows // 2, depth), F32)],
        compiler_params=params(),
        cost_estimate=cost(4e9, 16e6),
        name="images",
    )(mix, order, coef, steps, maps)
    return outs[:points], outs[points : 2 * points], outs[2 * points]


def rank_kernel(slots, mask_ref, place_ref, plane_ref, base_ref):
    sources, points, slab_rows, depth = mask_ref.shape
    rows = sources * slab_rows
    before = lax.broadcasted_iota(jnp.int32, (depth, depth), 0) < lax.broadcasted_iota(
        jnp.int32, (depth, depth), 1
    )
    above = lax.broadcasted_iota(jnp.int32, (rows, rows), 0)
    left = lax.broadcasted_iota(jnp.int32, (rows, rows), 1)
    same = left // slab_rows == above // slab_rows
    lower = ((left < above) & same).astype(BF16)
    upper = ((above < left) & same).astype(BF16)
    for t in range(points):
        mask = mask_ref[:, t].astype(F32).reshape(rows, depth)
        packed = mask.astype(BF16)
        within = jnp.dot(packed, before.astype(BF16), preferred_element_type=F32)
        totals = jnp.dot(packed, jnp.ones((depth, depth), BF16), preferred_element_type=F32)
        starts = jnp.dot(lower, totals.astype(BF16), preferred_element_type=F32)
        rank = within + starts
        place = rank - jnp.floor(rank * (1.0 / depth)) * depth
        place_ref[t] = jnp.where((mask > 0.0) & (rank < slots), place, -1.0)
        plane_ref[t] = packed
        across = lax.dot_general(
            jnp.ones((8, depth), BF16), packed, (((1,), (1,)), ((), ())), preferred_element_type=F32
        )
        base_ref[t] = jnp.dot(across.astype(BF16), upper, preferred_element_type=F32).astype(
            jnp.int32
        )


def rank_cells(mask_all, slots):
    sources, points, slab_rows, depth = mask_all.shape
    rows = sources * slab_rows
    return pl.pallas_call(
        functools.partial(rank_kernel, slots),
        out_shape=[
            jax.ShapeDtypeStruct((points, rows, depth), F32),
            jax.ShapeDtypeStruct((points, rows, depth), BF16),
            jax.ShapeDtypeStruct((points, 8, rows), jnp.int32),
        ],
        compiler_params=params(),
        cost_estimate=cost(1e8, 1e6),
        name="ranks",
    )(mask_all)


def data_kernel(full, shared, split, extra, table_ref, mask_ref, extra_ref, data_ref, *rest):
    main_ref, last_ref = rest[0], rest[1] if split else None
    chosen, kept_shared = rest[-2:]
    slab_rows, depth = mask_ref.shape[1:]
    together = data_ref.shape[0]
    dests, held, _ = main_ref.shape
    width = extra_ref.shape[1]
    tiles = full + shared
    t, group = pl.program_id(0), pl.program_id(1)
    coils = together * pl.num_programs(1)
    units = coils * full + (coils // 2) * shared

    @pl.when(group == 0)
    def choose():
        mask = mask_ref[0]
        before = lax.broadcasted_iota(jnp.int32, (depth, depth), 0) < lax.broadcasted_iota(
            jnp.int32, (depth, depth), 1
        )
        within = jnp.dot(mask, before.astype(BF16), preferred_element_type=F32)
        totals = jnp.dot(mask, jnp.ones((depth, depth), BF16), preferred_element_type=F32)
        slot = lax.broadcasted_iota(jnp.int32, (full * depth, depth), 0).astype(F32)
        side = lax.broadcasted_iota(jnp.int32, (depth, depth), 0)
        left = jnp.where(side < depth // 2, side + full * depth, -2).astype(F32)
        right = jnp.where(side < depth // 2, -2, side + full * depth - depth // 2).astype(F32)
        start = jnp.zeros((1, depth), F32)
        wide = mask.astype(F32)
        for k in range(slab_rows):
            rank = jnp.where(wide[k : k + 1] > 0.0, within[k : k + 1] + start, -1.0)
            at = slice(k * depth, (k + 1) * depth)
            chosen[: full * depth, at] = jnp.where(slot == rank, 1.0, 0.0).astype(BF16)
            if shared:
                chosen[full * depth : (full + 1) * depth, at] = jnp.where(
                    left == rank, 1.0, 0.0
                ).astype(BF16)
                chosen[(full + 1) * depth :, at] = jnp.where(right == rank, 1.0, 0.0).astype(BF16)
            start = start + totals[k : k + 1]
        for e in range(extra):
            main_ref[:, held - (extra - e) * width : held - (extra - e - 1) * width] = (
                jnp.broadcast_to(extra_ref[e][None], (dests, width, depth))
            )

    parts = []
    for c in range(together):
        data = jnp.swapaxes(data_ref[c, 0], 0, 1)
        cells = jnp.concatenate(
            [jnp.concatenate([data[2 * k], data[2 * k + 1]], axis=0) for k in range(slab_rows)],
            axis=1,
        )
        by_slot = (((1,), (1,)), ((), ()))
        kept = lax.dot_general(
            cells, chosen[: full * depth], by_slot, preferred_element_type=F32
        ).astype(BF16)
        if shared:
            end = chosen[(full + c) * depth : (full + c + 1) * depth]
            last = lax.dot_general(cells, end, by_slot, preferred_element_type=F32).astype(BF16)
            kept = jnp.concatenate([kept, last], axis=1)
        turned = jnp.dot(table_ref[...], kept, preferred_element_type=F32)
        parts.append(
            [
                turned[:, i * depth : (i + 1) * depth].reshape(dests, width, depth)
                for i in range(tiles)
            ]
        )
    if shared:
        parts.append([parts[0].pop() + parts[1].pop()])

    def put(ref, unit, value):
        start = pl.multiple_of(unit * width, width)
        ref[:, pl.ds(start, width)] = value.astype(BF16)

    @pl.when(t < pl.num_programs(0) - (1 if split else 0))
    def whole():
        for c in range(together):
            for i in range(full):
                put(main_ref, t * units + (group * together + c) * full + i, parts[c][i])
        if shared:
            put(main_ref, t * units + coils * full + group, parts[-1][0])

    if split:

        @pl.when(t == pl.num_programs(0) - 1)
        def halves():
            half = width // 2
            for ref, base, at in (
                (main_ref, t * units, slice(0, half)),
                (last_ref, 0, slice(half, width)),
            ):
                for i in range(full):
                    both = jnp.concatenate([parts[c][i][:, at] for c in range(2)], axis=1)
                    put(ref, base + group * full + i, both)
            if shared:
                kept_shared[group % 2] = parts[-1][0]

                @pl.when(group % 2 == 1)
                def pairs():
                    for ref, base, at in (
                        (main_ref, t * units, slice(0, half)),
                        (last_ref, 0, slice(half, width)),
                    ):
                        both = jnp.concatenate([kept_shared[p][:, at] for p in range(2)], axis=1)
                        put(ref, base + (coils // 2) * full + group // 2, both)


def transform_data(table, mask, extra, data, start, count, dests, fit, split):
    coils, points, first, rows2, depth = data.shape
    width = 2 * first // dests
    full, shared = fit
    together = 2 if coils % 2 == 0 else 1
    units = coils * full + (coils // 2) * shared
    more = 0 if start else extra.shape[0]
    held = [units * count - (units // 2 if split else 0) + more] + [units // 2] * split
    return pl.pallas_call(
        functools.partial(data_kernel, full, shared, split, more),
        grid=(count, coils // together),
        in_specs=[
            whole_block(table.shape),
            pl.BlockSpec((1, rows2 // 2, depth), lambda t, c: (start + t, 0, 0)),
            whole_block(extra.shape),
            pl.BlockSpec((together, 1, first, rows2, depth), lambda t, c: (c, start + t, 0, 0, 0)),
        ],
        out_specs=[whole_block((dests, n * width, depth)) for n in held],
        out_shape=[jax.ShapeDtypeStruct((dests, n * width, depth), BF16) for n in held],
        scratch_shapes=[
            pltpu.VMEM(((full + 2 * shared) * depth, rows2 // 2 * depth), BF16),
            pltpu.VMEM((2, dests, width, depth), F32),
        ],
        compiler_params=pltpu.CompilerParams(vmem_limit_bytes=56 * 2**20),
        cost_estimate=cost(2e9 * count, 8e6 * count),
        name="data",
    )(table, mask, extra, data)


def forward_kernel(depth_ref, row_ref, own_ref, far_ref, maps_ref, out_ref):
    coils, planes, _, rows, depth = maps_ref.shape
    pair = 2 if coils % 2 == 0 else 1
    @pl.loop(0, planes, unroll=math.gcd(planes, UNROLL))
    def one(x):
        real = own_ref[x, 0].astype(F32) + far_ref[x, 0].astype(F32)
        imaginary = own_ref[x, 1].astype(F32) + far_ref[x, 1].astype(F32)
        for c in range(0, coils, pair):
            stacked = []
            for k in range(c, c + pair):
                map_real = maps_ref[k, x, 0].astype(F32)
                map_imaginary = maps_ref[k, x, 1].astype(F32)
                coil_real = (map_real * real - map_imaginary * imaginary).astype(BF16)
                coil_imaginary = (map_real * imaginary + map_imaginary * real).astype(BF16)
                stacked.append(jnp.concatenate([coil_real, coil_imaginary], axis=1))
            deep = jnp.dot(
                jnp.concatenate(stacked, axis=0), depth_ref[...], preferred_element_type=F32
            ).astype(BF16)
            columns = [
                jnp.concatenate(
                    [
                        deep[k * rows : (k + 1) * rows, :depth],
                        deep[k * rows : (k + 1) * rows, depth:],
                    ],
                    axis=0,
                )
                for k in range(pair)
            ]
            lines = jnp.dot(
                row_ref[...], jnp.concatenate(columns, axis=1), preferred_element_type=F32
            )
            for k in range(pair):
                out_ref[c + k, x] = lines[:, k * depth : (k + 1) * depth].astype(BF16)


def forward_lines(depth_table, row_table, own, far, maps):
    coils, slab, _, rows, depth = maps.shape
    step = math.gcd(slab, PLANES)
    plane_block = pl.BlockSpec((step, 2, rows, depth), lambda x: (x, 0, 0, 0))
    return pl.pallas_call(
        forward_kernel,
        grid=(slab // step,),
        in_specs=[
            whole_block(depth_table.shape),
            whole_block(row_table.shape),
            plane_block,
            plane_block,
            pl.BlockSpec((coils, step, 2, rows, depth), lambda x: (0, x, 0, 0, 0)),
        ],
        out_specs=pl.BlockSpec((coils, step, 2 * rows, depth), lambda x: (0, x, 0, 0)),
        out_shape=jax.ShapeDtypeStruct((coils, slab, 2 * rows, depth), BF16),
        compiler_params=params(),
        cost_estimate=cost(3e9, 8e6),
        name="forward",
    )(depth_table, row_table, own, far, maps)


def back_kernel(
    spreads, fit, halved, depth_ref, row_ref, base_ref, place_ref, mask_ref, data_ref, lines_ref,
    maps_ref, phase_ref, out_ref, held, ready
):
    coils, planes = maps_ref.shape[:2]
    rows, depth = maps_ref.shape[3:]
    sources = data_ref.shape[0]
    full, shared = fit
    tiles = full + shared
    width = ready.shape[3]
    unit = 2 * width if halved else width
    high = coils * width
    step = pl.program_id(0)
    slab_rows = rows // (spreads * sources)

    def piece(s, u, part):
        value = data_ref[s, u * unit : (u + 1) * unit].astype(F32)
        return value[part * width : (part + 1) * width] if halved else value

    @pl.when(step < spreads)
    def spread():
        lane = lax.broadcasted_iota(jnp.int32, (high, depth), 1)
        slot = lax.broadcasted_iota(jnp.int32, (depth, depth), 0).astype(F32)
        @pl.loop(0, sources, unroll=math.gcd(sources, UNROLL))
        def one(s):
            for c in range(coils):
                for i in range(full):
                    if halved:
                        ready[s % 2, c, i] = piece(s, (c // 2) * full + i, c % 2)
                    else:
                        ready[s % 2, c, i] = piece(s, c * full + i, 0)
                if shared:
                    if halved:
                        last = piece(s, (coils // 2) * full + c // 4, (c // 2) % 2)
                    else:
                        last = piece(s, coils * full + c // 2, 0)
                    ready[s % 2, c, full] = pltpu.roll(last, depth // 2, 1) if c % 2 else last
            first = pl.multiple_of((step * sources + s) * slab_rows, slab_rows)
            sides = []
            for k in range(slab_rows):
                base = base_ref[first + k]
                at = jnp.minimum(base // depth, tiles - 1)
                after = jnp.minimum(at + 1, tiles - 1)
                low = ready[s % 2, :, at].reshape(high, depth)
                top = ready[s % 2, :, after].reshape(high, depth)
                sides.append(jnp.where(lane >= base % depth, low, top).astype(BF16))
            places = place_ref[0, pl.ds(first, slab_rows), :]
            spread_out = [
                jnp.dot(
                    sides[k],
                    jnp.where(slot == places[k : k + 1], 1.0, 0.0).astype(BF16),
                    preferred_element_type=F32,
                )
                for k in range(slab_rows)
            ]
            span = slab_rows * high
            held[pl.ds(pl.multiple_of(first * high, span), span), :] = jnp.concatenate(
                spread_out, axis=0
            )

    @pl.when(step >= spreads)
    def back():
        pair = 2 if coils % 2 == 0 else 1
        mask = mask_ref[0].astype(F32)
        mask = jnp.concatenate([mask, mask], axis=0)
        @pl.loop(0, planes, unroll=math.gcd(planes, UNROLL))
        def one(j):
            x = (step - spreads) * planes + j
            sum_real = sum_imaginary = None
            for c in range(0, coils, pair):
                columns = []
                for k in range(c, c + pair):
                    parts = [
                        held[pl.ds(k * width + 2 * x + p, rows, stride=high), :] for p in range(2)
                    ]
                    columns.append(
                        (lines_ref[k, j].astype(F32) * mask - jnp.concatenate(parts, axis=0)).astype(BF16)
                    )
                turned = jnp.dot(
                    row_ref[...], jnp.concatenate(columns, axis=1), preferred_element_type=F32
                ).astype(BF16)
                stacked = []
                for k in range(pair):
                    part = turned[:, k * depth : (k + 1) * depth]
                    stacked.append(jnp.concatenate([part[:rows], part[rows:]], axis=1))
                images = jnp.dot(
                    jnp.concatenate(stacked, axis=0), depth_ref[...], preferred_element_type=F32
                )
                for k in range(pair):
                    map_real = maps_ref[c + k, j, 0].astype(F32)
                    map_imaginary = maps_ref[c + k, j, 1].astype(F32)
                    back_real = images[k * rows : (k + 1) * rows, :depth]
                    back_imaginary = images[k * rows : (k + 1) * rows, depth:]
                    term_real = map_real * back_real + map_imaginary * back_imaginary
                    term_imaginary = map_real * back_imaginary - map_imaginary * back_real
                    sum_real = term_real if sum_real is None else sum_real + term_real
                    sum_imaginary = (
                        term_imaginary if sum_imaginary is None else sum_imaginary + term_imaginary
                    )
            cosine, sine = phase_ref[j, 0], phase_ref[j, 1]
            out_ref[j, 0] = (cosine * sum_real + sine * sum_imaginary).astype(BF16)
            out_ref[j, 1] = (cosine * sum_imaginary - sine * sum_real).astype(BF16)


def back_images(depth_table, row_table, ranks, data, lines, maps, phase, t, place_in, fit):
    coils, slab, _, rows, depth = maps.shape
    place, mask, base = ranks
    sources = data.shape[0]
    full, shared = fit
    unit, start, planes = place_in
    halved = planes < slab
    width = 2 * planes
    units = (coils * full + (coils // 2) * shared) // (2 if halved else 1)
    block_rows = units * 2 * slab
    step = math.gcd(planes, BACK_PLANES)
    some = math.gcd(sources, SOURCES)
    spreads = sources // some

    def plane(i):
        return jnp.maximum(i - spreads, 0)

    def from_whole(i):
        return start // step + plane(i)

    return pl.pallas_call(
        functools.partial(back_kernel, spreads, fit, halved),
        grid=(spreads + planes // step,),
        in_specs=[
            whole_block(depth_table.shape),
            whole_block(row_table.shape),
            pl.BlockSpec(memory_space=pltpu.SMEM),
            pl.BlockSpec((1, rows, depth), lambda i: (t, 0, 0)),
            pl.BlockSpec((1, rows, depth), lambda i: (t, 0, 0)),
            pl.BlockSpec(
                (some, block_rows, depth),
                lambda i: (jnp.minimum(i, spreads - 1), unit // units, 0),
            ),
            pl.BlockSpec((coils, step, 2 * rows, depth), lambda i: (0, from_whole(i), 0, 0)),
            pl.BlockSpec((coils, step, 2, rows, depth), lambda i: (0, from_whole(i), 0, 0, 0)),
            pl.BlockSpec((step, 2, rows, depth), lambda i: (from_whole(i), 0, 0, 0)),
        ],
        out_specs=pl.BlockSpec((step, 2, rows, depth), lambda i: (plane(i), 0, 0, 0)),
        out_shape=jax.ShapeDtypeStruct((planes, 2, rows, depth), BF16),
        scratch_shapes=[
            pltpu.VMEM((rows * coils * width, depth), F32),
            pltpu.VMEM((2, coils, full + shared, width, depth), F32),
        ],
        compiler_params=params(),
        cost_estimate=cost(3e9, 10e6),
        name="back",
    )(depth_table, row_table, base[t, 0], place, mask, data, lines, maps, phase)


def gradient_kernel(points, halves, block, mix_ref, *rest):
    out_ref = rest[-1]
    ranks, planes, rows2, depth = out_ref.shape
    count = points - 1 + halves
    own_refs, far_refs = rest[:count], rest[count : 2 * count]

    def fill(last):
        chosen = [*range(points - 1), last]
        @pl.loop(0, planes, unroll=math.gcd(planes, UNROLL))
        def one(x):
            for i in range(rows2 // (2 * block)):
                at = slice(i * block, (i + 1) * block)
                columns = [
                    jnp.concatenate([refs[k][x, p, at, :] for k in chosen for p in range(2)], axis=0)
                    for refs in (own_refs, far_refs)
                ]
                both = jnp.dot(
                    mix_ref[...], jnp.concatenate(columns, axis=1), preferred_element_type=F32
                )
                total = both[:, :depth] + both[:, depth:]
                out_ref[:, x, 2 * i * block : 2 * (i + 1) * block, :] = total.reshape(
                    ranks, 2 * block, depth
                )

    if halves == 1:
        fill(points - 1)
    else:
        middle = pl.num_programs(0) // 2
        pl.when(pl.program_id(0) < middle)(lambda: fill(points - 1))
        pl.when(pl.program_id(0) >= middle)(lambda: fill(points))


def gradient(mix, own, far, ranks, points):
    slab, _, rows, depth = own[0].shape
    halves = len(own) - points + 1
    step = math.gcd(slab // halves, GRADIENT_PLANES)
    middle = slab // (2 * step)
    shape = (step, 2, rows, depth)
    blocks = [pl.BlockSpec(shape, lambda x: (x, 0, 0, 0))] * (points if halves == 1 else points - 1)
    if halves == 2:
        blocks.append(pl.BlockSpec(shape, lambda x: (jnp.minimum(x, middle - 1), 0, 0, 0)))
        blocks.append(pl.BlockSpec(shape, lambda x: (jnp.maximum(x - middle, 0), 0, 0, 0)))
    return pl.pallas_call(
        functools.partial(gradient_kernel, points, halves, mix.shape[1] // (2 * points)),
        grid=(slab // step,),
        in_specs=[whole_block(mix.shape)] + blocks * 2,
        out_specs=pl.BlockSpec((ranks, step, 2 * rows, depth), lambda x: (0, x, 0, 0)),
        out_shape=jax.ShapeDtypeStruct((ranks, slab, 2 * rows, depth), F32),
        compiler_params=params(),
        cost_estimate=cost(4e9, 12e6),
        name="gradient",
    )(mix, *own, *far)


def from_other_groups(part, axis):
    groups = lax.axis_size(axis)
    moved = [
        lax.ppermute(part, axis, [(g, (g + shift) % groups) for g in range(groups)])
        for shift in range(1, groups)
    ]
    if groups == 1:
        return jnp.zeros_like(part)
    if groups == 2:
        return moved[0]
    return sum(m.astype(F32) for m in moved).astype(BF16)


def shards(spatial_coef, temporal_basis, coil_maps, field_steps, kspace_data, sample_mask):
    points = temporal_basis.shape[2]
    ranks, slab, rows, _, depth = spatial_coef.shape
    coils = coil_maps.shape[0]
    first, slab_rows = kspace_data.shape[2:4]
    dests = lax.axis_size("space")
    basis = lax.dynamic_slice_in_dim(
        temporal_basis, lax.axis_index("coil") * ranks, ranks, axis=1
    )
    mix, adjoint = mix_factors(basis, 16, False), mix_factors(basis, 32, True)
    data = kspace_data.reshape(coils, points, first, 2 * slab_rows, depth)
    maps = coil_maps.reshape(coils, slab, 2 * rows, depth)
    coef = spatial_coef.reshape(ranks, slab, 2 * rows, depth)
    cells = slab_rows * depth
    half_tiles = -(-SENT_SIXTEENTHS * cells // (8 * depth))
    if coils % 2:
        half_tiles += half_tiles % 2
    fit = (half_tiles // 2, half_tiles % 2)
    slots = half_tiles * depth // 2
    width = 2 * first // dests
    mask_here = sample_mask.astype(BF16)
    held = -(-points * slab_rows // width)
    extra = jnp.pad(
        mask_here.reshape(points * slab_rows, depth),
        ((0, held * width - points * slab_rows), (0, 0)),
    ).reshape(held, width, depth)
    first_table = real_table(first, 1.0, out_interleaved=True)
    depth_forward, depth_back = real_table(depth, -1.0).T, real_table(depth, 1.0).T
    rows_forward, rows_back = real_table(rows, -1.0), real_table(rows, 1.0)

    def prepare(data, start, count, split=False):
        return transform_data(
            first_table, mask_here, extra, data, start, count, dests, fit, split
        )

    def send(sent):
        return lax.all_to_all(sent, "space", split_axis=0, concat_axis=0, tiled=True)

    def back(piece, arrived, lines):
        t, chunk, unit, start, planes_here = piece
        own = back_images(
            depth_back, rows_back, ranked, arrived[chunk], lines[t], planes, phases[t], t,
            (unit, start, planes_here), fit,
        )
        return own, from_other_groups(own, "coil")

    units = coils * fit[0] + (coils // 2) * fit[1]
    head = min(HEAD, points)
    split = points > head and coils % 4 == 0 and slab % 8 == 0
    pieces = [(t, 0, t * units, 0, slab) for t in range(head)]
    pieces += [(t, 1, (t - head) * units, 0, slab) for t in range(head, points)]
    if split:
        last = (points - 1 - head) * units
        pieces[-1] = (points - 1, 1, last, 0, slab // 2)
        pieces.append((points - 1, 2, 0, slab // 2, slab // 2))

    sent = prepare(data, 0, head)
    arrived = [send(sent[0])]
    coef, _ = lax.optimization_barrier((coef, sent[0]))
    turned, phases, planes = make_images(mix, coef, field_steps, maps, points)
    others = [from_other_groups(part, "coil") for part in turned]
    lines = [
        forward_lines(depth_forward, rows_forward, turned[t], others[t], planes)
        for t in range(points)
    ]
    if points > head:
        data, _ = lax.optimization_barrier((data, planes))
        sent = prepare(data, head, points - head, split)
        sent, _ = lax.optimization_barrier((sent, lines[: points - 1]))
        arrived.append(send(sent[0]))
    mask_all = arrived[0][:, head * units * width :].reshape(dests, held * width, depth)
    mask_all = mask_all[:, : points * slab_rows].reshape(dests, points, slab_rows, depth)
    ranked = rank_cells(mask_all, slots)
    early = [back(piece, arrived, lines) for piece in pieces if piece[1] == 0]

    def finish(early, lines, arrived, sent):
        arrived = arrived + [send(part) for part in sent[1:]]
        done = early + [back(piece, arrived, lines) for piece in pieces[len(early) :]]
        own, far = zip(*done)
        return gradient(adjoint, own, far, ranks, points)

    def finish_more(early, lines, arrived, sent):
        count = jnp.cumsum(mask_here.astype(F32).reshape(points, cells), axis=1)
        rest = jnp.where(count > slots, mask_here.reshape(points, cells), 0).astype(BF16)
        rest = rest.reshape(1, points, 1, slab_rows, 1, depth)
        table = real_table(first, 1.0).reshape(2, first, 2, first)
        moved = jnp.einsum(
            "ctxypz,qkpx->ctkqyz", kspace_data * rest, table, preferred_element_type=F32
        ).astype(BF16)
        moved = lax.all_to_all(moved, "space", split_axis=2, concat_axis=4, tiled=True)
        moved = moved.reshape(coils, points, slab, 2 * rows, depth)
        lines = [
            (lines[t].astype(F32) - moved[:, t].astype(F32)).astype(BF16) for t in range(points)
        ]
        early = [back(piece, arrived, lines) for piece in pieces[: len(early)]]
        return finish(early, lines, arrived, sent)

    most = jnp.max(jnp.sum(mask_all.astype(F32), axis=(2, 3)))
    result = lax.cond(most > slots, finish_more, finish, early, lines, arrived, sent)
    return result.reshape(ranks, slab, rows, 2, depth)


def solution(mesh):
    in_specs = (
        P("coil", "space", None, None, None),
        P(),
        P("coil", "space", None, None, None),
        P("space", None, None),
        P("coil", None, None, "space", None, None),
        P(None, "space", None),
    )
    out_specs = P("coil", "space", None, None, None)
    return jax.shard_map(shards, mesh=mesh, in_specs=in_specs, out_specs=out_specs, check_vma=False)
```

```python
import functools
import math

import jax
import jax.numpy as jnp
import ml_dtypes
import numpy as np
from jax import lax
from jax.experimental import pallas as pl
from jax.experimental.pallas import tpu as pltpu
from jax.sharding import PartitionSpec as P

STEPS_CYCLE = 256
SENT_SIXTEENTHS = 9
PLANES = 4
BACK_PLANES = 8
SOURCES = 8
HEAD = 2
IMAGE_UNROLL = 1
FORWARD_UNROLL = 2
BACK_UNROLL = 2
GRADIENT_PLANES = 2
VMEM_BYTES = 24 * 2**20
F32 = jnp.float32
BF16 = jnp.bfloat16


def real_table(length, sign, out_interleaved=False):
    index = np.arange(length)
    angle = (index[:, None] * index[None, :] % length) * (2.0 * math.pi / length)
    cosine = np.cos(angle) / math.sqrt(length)
    sine = sign * np.sin(angle) / math.sqrt(length)
    table = np.block([[cosine, -sine], [sine, cosine]])
    if out_interleaved:
        table = table.reshape(2, length, 2 * length).swapaxes(0, 1).reshape(2 * length, 2 * length)
    return jnp.asarray(table.astype(np.float32).astype(ml_dtypes.bfloat16))


def params():
    return pltpu.CompilerParams(vmem_limit_bytes=VMEM_BYTES)


def cost(flops, moved):
    return pl.CostEstimate(flops=int(flops), bytes_accessed=int(moved), transcendentals=0)


def whole_block(shape):
    return pl.BlockSpec(shape, lambda *_: (0,) * len(shape))


def unit_turn(steps):
    x = ((steps & (STEPS_CYCLE - 1)) - STEPS_CYCLE // 2).astype(F32) * (2.0 * math.pi / STEPS_CYCLE)
    square = x * x
    cosine = jnp.zeros_like(x)
    sine = jnp.zeros_like(x)
    for k in range(9, -1, -1):
        cosine = cosine * square + (-1.0) ** k / math.factorial(2 * k)
        sine = sine * square + (-1.0) ** k / math.factorial(2 * k + 1)
    return -cosine, -sine * x


def mix_factors(basis, block, interleaved):
    real, imaginary = basis[0], basis[1]
    eye = jnp.eye(block, dtype=basis.dtype)
    forward = jnp.stack([jnp.stack([real, -imaginary]), jnp.stack([imaginary, real])])
    adjoint = jnp.stack([jnp.stack([real, imaginary]), jnp.stack([-imaginary, real])])
    ranks, points = real.shape
    if interleaved:
        return jnp.einsum("qplt,yz->lyqtpz", adjoint, eye).reshape(
            ranks * block * 2, points * 2 * block
        )
    return jnp.einsum("qplt,yz->tqylzp", forward, eye).reshape(
        points * 2 * block, ranks * block * 2
    )


def image_kernel(points, block, mix_ref, order_ref, coef_ref, steps_ref, maps_ref, *rest):
    turned_refs, phase_refs = rest[:points], rest[points : 2 * points]
    planes_ref, mixed = rest[2 * points :]
    ranks, planes, rows2, depth = coef_ref.shape
    coils = maps_ref.shape[0]
    rows = rows2 // 2
    blocks = rows // block
    @pl.loop(0, planes, unroll=math.gcd(planes, IMAGE_UNROLL))
    def one(x):
        pair = 2 if blocks % 2 == 0 else 1
        for i in range(0, blocks, pair):
            columns = [
                jnp.concatenate(
                    [coef_ref[l, x, 2 * block * k : 2 * block * (k + 1), :] for l in range(ranks)],
                    axis=0,
                )
                for k in range(i, i + pair)
            ]
            image = jnp.dot(
                mix_ref[...], jnp.concatenate(columns, axis=1), preferred_element_type=F32
            )
            for k in range(pair):
                for j in range(2 * points):
                    mixed[j, (i + k) * block : (i + k + 1) * block, :] = image[
                        j * block : (j + 1) * block, k * depth : (k + 1) * depth
                    ]
        cosine, sine = unit_turn(steps_ref[x])
        now_cosine, now_sine = cosine, sine
        for t in range(points):
            if t:
                now_cosine, now_sine = (
                    now_cosine * cosine - now_sine * sine,
                    now_sine * cosine + now_cosine * sine,
                )
            real, imaginary = mixed[2 * t], mixed[2 * t + 1]
            turned_refs[t][x, 0] = (now_cosine * real - now_sine * imaginary).astype(BF16)
            turned_refs[t][x, 1] = (now_sine * real + now_cosine * imaginary).astype(BF16)
            phase_refs[t][x, 0] = now_cosine
            phase_refs[t][x, 1] = now_sine
        pair = 2 if coils % 2 == 0 else 1
        for c in range(0, coils, pair):
            both = jnp.concatenate([maps_ref[c + k, x] for k in range(pair)], axis=1)
            parted = jnp.dot(order_ref[...], both, preferred_element_type=F32).astype(BF16)
            for k in range(pair):
                planes_ref[c + k, x] = parted[:, k * depth : (k + 1) * depth].reshape(
                    2, rows, depth
                )


def make_images(mix, coef, steps, maps, points):
    ranks, slab, rows, depth = coef.shape
    coils = maps.shape[0]
    step = math.gcd(slab, PLANES)
    plane = (2, rows // 2, depth)
    plane_block = pl.BlockSpec((step,) + plane, lambda x: (x, 0, 0, 0))
    order = np.eye(rows, dtype=np.float32).reshape(rows // 2, 2, rows).swapaxes(0, 1)
    order = jnp.asarray(order.reshape(rows, rows).astype(ml_dtypes.bfloat16))
    outs = pl.pallas_call(
        functools.partial(image_kernel, points, mix.shape[0] // (2 * points)),
        grid=(slab // step,),
        in_specs=[
            whole_block(mix.shape),
            whole_block(order.shape),
            pl.BlockSpec((ranks, step, rows, depth), lambda x: (0, x, 0, 0)),
            pl.BlockSpec((step, rows // 2, depth), lambda x: (x, 0, 0)),
            pl.BlockSpec((coils, step, rows, depth), lambda x: (0, x, 0, 0)),
        ],
        out_specs=[plane_block] * (2 * points)
        + [pl.BlockSpec((coils, step) + plane, lambda x: (0, x, 0, 0, 0))],
        out_shape=[jax.ShapeDtypeStruct((slab,) + plane, BF16)] * points
        + [jax.ShapeDtypeStruct((slab,) + plane, F32)] * points
        + [jax.ShapeDtypeStruct((coils, slab) + plane, BF16)],
        scratch_shapes=[pltpu.VMEM((2 * points, rows // 2, depth), F32)],
        compiler_params=params(),
        cost_estimate=cost(4e9, 16e6),
        name="images",
    )(mix, order, coef, steps, maps)
    return outs[:points], outs[points : 2 * points], outs[2 * points]


def rank_kernel(slots, mask_ref, place_ref, plane_ref, base_ref):
    sources, points, slab_rows, depth = mask_ref.shape
    rows = sources * slab_rows
    before = lax.broadcasted_iota(jnp.int32, (depth, depth), 0) < lax.broadcasted_iota(
        jnp.int32, (depth, depth), 1
    )
    above = lax.broadcasted_iota(jnp.int32, (rows, rows), 0)
    left = lax.broadcasted_iota(jnp.int32, (rows, rows), 1)
    same = left // slab_rows == above // slab_rows
    lower = ((left < above) & same).astype(BF16)
    upper = ((above < left) & same).astype(BF16)
    for t in range(points):
        mask = mask_ref[:, t].astype(F32).reshape(rows, depth)
        packed = mask.astype(BF16)
        within = jnp.dot(packed, before.astype(BF16), preferred_element_type=F32)
        totals = jnp.dot(packed, jnp.ones((depth, depth), BF16), preferred_element_type=F32)
        starts = jnp.dot(lower, totals.astype(BF16), preferred_element_type=F32)
        rank = within + starts
        place = rank - jnp.floor(rank * (1.0 / depth)) * depth
        place_ref[t] = jnp.where((mask > 0.0) & (rank < slots), place, -1.0)
        plane_ref[t] = packed
        across = lax.dot_general(
            jnp.ones((8, depth), BF16), packed, (((1,), (1,)), ((), ())), preferred_element_type=F32
        )
        base_ref[t] = jnp.dot(across.astype(BF16), upper, preferred_element_type=F32).astype(
            jnp.int32
        )


def rank_cells(mask_all, slots):
    sources, points, slab_rows, depth = mask_all.shape
    rows = sources * slab_rows
    return pl.pallas_call(
        functools.partial(rank_kernel, slots),
        out_shape=[
            jax.ShapeDtypeStruct((points, rows, depth), F32),
            jax.ShapeDtypeStruct((points, rows, depth), BF16),
            jax.ShapeDtypeStruct((points, 8, rows), jnp.int32),
        ],
        compiler_params=params(),
        cost_estimate=cost(1e8, 1e6),
        name="ranks",
    )(mask_all)


def data_kernel(full, shared, split, extra, table_ref, mask_ref, extra_ref, data_ref, *rest):
    main_ref, last_ref = rest[0], rest[1] if split else None
    chosen, kept_shared = rest[-2:]
    slab_rows, depth = mask_ref.shape[1:]
    together = data_ref.shape[0]
    dests, held, _ = main_ref.shape
    width = extra_ref.shape[1]
    tiles = full + shared
    t, group = pl.program_id(0), pl.program_id(1)
    coils = together * pl.num_programs(1)
    units = coils * full + (coils // 2) * shared

    @pl.when(group == 0)
    def choose():
        mask = mask_ref[0]
        before = lax.broadcasted_iota(jnp.int32, (depth, depth), 0) < lax.broadcasted_iota(
            jnp.int32, (depth, depth), 1
        )
        within = jnp.dot(mask, before.astype(BF16), preferred_element_type=F32)
        totals = jnp.dot(mask, jnp.ones((depth, depth), BF16), preferred_element_type=F32)
        slot = lax.broadcasted_iota(jnp.int32, (full * depth, depth), 0).astype(F32)
        side = lax.broadcasted_iota(jnp.int32, (depth, depth), 0)
        left = jnp.where(side < depth // 2, side + full * depth, -2).astype(F32)
        right = jnp.where(side < depth // 2, -2, side + full * depth - depth // 2).astype(F32)
        start = jnp.zeros((1, depth), F32)
        wide = mask.astype(F32)
        for k in range(slab_rows):
            rank = jnp.where(wide[k : k + 1] > 0.0, within[k : k + 1] + start, -1.0)
            at = slice(k * depth, (k + 1) * depth)
            chosen[: full * depth, at] = jnp.where(slot == rank, 1.0, 0.0).astype(BF16)
            if shared:
                chosen[full * depth : (full + 1) * depth, at] = jnp.where(
                    left == rank, 1.0, 0.0
                ).astype(BF16)
                chosen[(full + 1) * depth :, at] = jnp.where(right == rank, 1.0, 0.0).astype(BF16)
            start = start + totals[k : k + 1]
        for e in range(extra):
            main_ref[:, held - (extra - e) * width : held - (extra - e - 1) * width] = (
                jnp.broadcast_to(extra_ref[e][None], (dests, width, depth))
            )

    parts = []
    for c in range(together):
        data = jnp.swapaxes(data_ref[c, 0], 0, 1)
        cells = jnp.concatenate(
            [jnp.concatenate([data[2 * k], data[2 * k + 1]], axis=0) for k in range(slab_rows)],
            axis=1,
        )
        by_slot = (((1,), (1,)), ((), ()))
        kept = lax.dot_general(
            cells, chosen[: full * depth], by_slot, preferred_element_type=F32
        ).astype(BF16)
        if shared:
            end = chosen[(full + c) * depth : (full + c + 1) * depth]
            last = lax.dot_general(cells, end, by_slot, preferred_element_type=F32).astype(BF16)
            kept = jnp.concatenate([kept, last], axis=1)
        turned = jnp.dot(table_ref[...], kept, preferred_element_type=F32)
        parts.append(
            [
                turned[:, i * depth : (i + 1) * depth].reshape(dests, width, depth)
                for i in range(tiles)
            ]
        )
    if shared:
        parts.append([parts[0].pop() + parts[1].pop()])

    def put(ref, unit, value):
        start = pl.multiple_of(unit * width, width)
        ref[:, pl.ds(start, width)] = value.astype(BF16)

    @pl.when(t < pl.num_programs(0) - (1 if split else 0))
    def whole():
        for c in range(together):
            for i in range(full):
                put(main_ref, t * units + (group * together + c) * full + i, parts[c][i])
        if shared:
            put(main_ref, t * units + coils * full + group, parts[-1][0])

    if split:

        @pl.when(t == pl.num_programs(0) - 1)
        def halves():
            half = width // 2
            for ref, base, at in (
                (main_ref, t * units, slice(0, half)),
                (last_ref, 0, slice(half, width)),
            ):
                for i in range(full):
                    both = jnp.concatenate([parts[c][i][:, at] for c in range(2)], axis=1)
                    put(ref, base + group * full + i, both)
            if shared:
                kept_shared[group % 2] = parts[-1][0]

                @pl.when(group % 2 == 1)
                def pairs():
                    for ref, base, at in (
                        (main_ref, t * units, slice(0, half)),
                        (last_ref, 0, slice(half, width)),
                    ):
                        both = jnp.concatenate([kept_shared[p][:, at] for p in range(2)], axis=1)
                        put(ref, base + (coils // 2) * full + group // 2, both)


def transform_data(table, mask, extra, data, start, count, dests, fit, split):
    coils, points, first, rows2, depth = data.shape
    width = 2 * first // dests
    full, shared = fit
    together = 2 if coils % 2 == 0 else 1
    units = coils * full + (coils // 2) * shared
    more = 0 if start else extra.shape[0]
    held = [units * count - (units // 2 if split else 0) + more] + [units // 2] * split
    return pl.pallas_call(
        functools.partial(data_kernel, full, shared, split, more),
        grid=(count, coils // together),
        in_specs=[
            whole_block(table.shape),
            pl.BlockSpec((1, rows2 // 2, depth), lambda t, c: (start + t, 0, 0)),
            whole_block(extra.shape),
            pl.BlockSpec((together, 1, first, rows2, depth), lambda t, c: (c, start + t, 0, 0, 0)),
        ],
        out_specs=[whole_block((dests, n * width, depth)) for n in held],
        out_shape=[jax.ShapeDtypeStruct((dests, n * width, depth), BF16) for n in held],
        scratch_shapes=[
            pltpu.VMEM(((full + 2 * shared) * depth, rows2 // 2 * depth), BF16),
            pltpu.VMEM((2, dests, width, depth), F32),
        ],
        compiler_params=pltpu.CompilerParams(vmem_limit_bytes=56 * 2**20),
        cost_estimate=cost(2e9 * count, 8e6 * count),
        name="data",
    )(table, mask, extra, data)


def forward_kernel(depth_ref, row_ref, own_ref, far_ref, maps_ref, out_ref):
    coils, planes, _, rows, depth = maps_ref.shape
    pair = 2 if coils % 2 == 0 else 1
    @pl.loop(0, planes, unroll=math.gcd(planes, FORWARD_UNROLL))
    def one(x):
        real = own_ref[x, 0].astype(F32) + far_ref[x, 0].astype(F32)
        imaginary = own_ref[x, 1].astype(F32) + far_ref[x, 1].astype(F32)
        for c in range(0, coils, pair):
            stacked = []
            for k in range(c, c + pair):
                map_real = maps_ref[k, x, 0].astype(F32)
                map_imaginary = maps_ref[k, x, 1].astype(F32)
                coil_real = (map_real * real - map_imaginary * imaginary).astype(BF16)
                coil_imaginary = (map_real * imaginary + map_imaginary * real).astype(BF16)
                stacked.append(jnp.concatenate([coil_real, coil_imaginary], axis=1))
            deep = jnp.dot(
                jnp.concatenate(stacked, axis=0), depth_ref[...], preferred_element_type=F32
            ).astype(BF16)
            columns = [
                jnp.concatenate(
                    [
                        deep[k * rows : (k + 1) * rows, :depth],
                        deep[k * rows : (k + 1) * rows, depth:],
                    ],
                    axis=0,
                )
                for k in range(pair)
            ]
            lines = jnp.dot(
                row_ref[...], jnp.concatenate(columns, axis=1), preferred_element_type=F32
            )
            for k in range(pair):
                out_ref[c + k, x] = lines[:, k * depth : (k + 1) * depth].astype(BF16)


def forward_lines(depth_table, row_table, own, far, maps):
    coils, slab, _, rows, depth = maps.shape
    step = math.gcd(slab, PLANES)
    plane_block = pl.BlockSpec((step, 2, rows, depth), lambda x: (x, 0, 0, 0))
    return pl.pallas_call(
        forward_kernel,
        grid=(slab // step,),
        in_specs=[
            whole_block(depth_table.shape),
            whole_block(row_table.shape),
            plane_block,
            plane_block,
            pl.BlockSpec((coils, step, 2, rows, depth), lambda x: (0, x, 0, 0, 0)),
        ],
        out_specs=pl.BlockSpec((coils, step, 2 * rows, depth), lambda x: (0, x, 0, 0)),
        out_shape=jax.ShapeDtypeStruct((coils, slab, 2 * rows, depth), BF16),
        compiler_params=params(),
        cost_estimate=cost(3e9, 8e6),
        name="forward",
    )(depth_table, row_table, own, far, maps)


def back_kernel(
    spreads, fit, halved, depth_ref, row_ref, base_ref, place_ref, mask_ref, data_ref, lines_ref,
    maps_ref, phase_ref, out_ref, held, ready
):
    coils, planes = maps_ref.shape[:2]
    rows, depth = maps_ref.shape[3:]
    sources = data_ref.shape[0]
    full, shared = fit
    tiles = full + shared
    width = ready.shape[3]
    unit = 2 * width if halved else width
    high = coils * width
    step = pl.program_id(0)
    slab_rows = rows // (spreads * sources)

    def piece(s, u, part):
        value = data_ref[s, u * unit : (u + 1) * unit].astype(F32)
        return value[part * width : (part + 1) * width] if halved else value

    @pl.when(step < spreads)
    def spread():
        lane = lax.broadcasted_iota(jnp.int32, (high, depth), 1)
        slot = lax.broadcasted_iota(jnp.int32, (depth, depth), 0).astype(F32)
        @pl.loop(0, sources, unroll=math.gcd(sources, BACK_UNROLL))
        def one(s):
            for c in range(coils):
                for i in range(full):
                    if halved:
                        ready[s % 2, c, i] = piece(s, (c // 2) * full + i, c % 2)
                    else:
                        ready[s % 2, c, i] = piece(s, c * full + i, 0)
                if shared:
                    if halved:
                        last = piece(s, (coils // 2) * full + c // 4, (c // 2) % 2)
                    else:
                        last = piece(s, coils * full + c // 2, 0)
                    ready[s % 2, c, full] = pltpu.roll(last, depth // 2, 1) if c % 2 else last
            first = pl.multiple_of((step * sources + s) * slab_rows, slab_rows)
            sides = []
            for k in range(slab_rows):
                base = base_ref[first + k]
                at = jnp.minimum(base // depth, tiles - 1)
                after = jnp.minimum(at + 1, tiles - 1)
                low = ready[s % 2, :, at].reshape(high, depth)
                top = ready[s % 2, :, after].reshape(high, depth)
                sides.append(jnp.where(lane >= base % depth, low, top).astype(BF16))
            places = place_ref[0, pl.ds(first, slab_rows), :]
            spread_out = [
                jnp.dot(
                    sides[k],
                    jnp.where(slot == places[k : k + 1], 1.0, 0.0).astype(BF16),
                    preferred_element_type=F32,
                )
                for k in range(slab_rows)
            ]
            span = slab_rows * high
            held[pl.ds(pl.multiple_of(first * high, span), span), :] = jnp.concatenate(
                spread_out, axis=0
            )

    @pl.when(step >= spreads)
    def back():
        pair = 2 if coils % 2 == 0 else 1
        mask = mask_ref[0].astype(F32)
        mask = jnp.concatenate([mask, mask], axis=0)
        @pl.loop(0, planes, unroll=math.gcd(planes, BACK_UNROLL))
        def one(j):
            x = (step - spreads) * planes + j
            sum_real = sum_imaginary = None
            for c in range(0, coils, pair):
                columns = []
                for k in range(c, c + pair):
                    parts = [
                        held[pl.ds(k * width + 2 * x + p, rows, stride=high), :] for p in range(2)
                    ]
                    columns.append(
                        (lines_ref[k, j].astype(F32) * mask - jnp.concatenate(parts, axis=0)).astype(BF16)
                    )
                turned = jnp.dot(
                    row_ref[...], jnp.concatenate(columns, axis=1), preferred_element_type=F32
                ).astype(BF16)
                stacked = []
                for k in range(pair):
                    part = turned[:, k * depth : (k + 1) * depth]
                    stacked.append(jnp.concatenate([part[:rows], part[rows:]], axis=1))
                images = jnp.dot(
                    jnp.concatenate(stacked, axis=0), depth_ref[...], preferred_element_type=F32
                )
                for k in range(pair):
                    map_real = maps_ref[c + k, j, 0].astype(F32)
                    map_imaginary = maps_ref[c + k, j, 1].astype(F32)
                    back_real = images[k * rows : (k + 1) * rows, :depth]
                    back_imaginary = images[k * rows : (k + 1) * rows, depth:]
                    term_real = map_real * back_real + map_imaginary * back_imaginary
                    term_imaginary = map_real * back_imaginary - map_imaginary * back_real
                    sum_real = term_real if sum_real is None else sum_real + term_real
                    sum_imaginary = (
                        term_imaginary if sum_imaginary is None else sum_imaginary + term_imaginary
                    )
            cosine, sine = phase_ref[j, 0], phase_ref[j, 1]
            out_ref[j, 0] = (cosine * sum_real + sine * sum_imaginary).astype(BF16)
            out_ref[j, 1] = (cosine * sum_imaginary - sine * sum_real).astype(BF16)


def back_images(depth_table, row_table, ranks, data, lines, maps, phase, t, place_in, fit):
    coils, slab, _, rows, depth = maps.shape
    place, mask, base = ranks
    sources = data.shape[0]
    full, shared = fit
    unit, start, planes = place_in
    halved = planes < slab
    width = 2 * planes
    units = (coils * full + (coils // 2) * shared) // (2 if halved else 1)
    block_rows = units * 2 * slab
    step = math.gcd(planes, BACK_PLANES)
    some = math.gcd(sources, SOURCES)
    spreads = sources // some

    def plane(i):
        return jnp.maximum(i - spreads, 0)

    def from_whole(i):
        return start // step + plane(i)

    return pl.pallas_call(
        functools.partial(back_kernel, spreads, fit, halved),
        grid=(spreads + planes // step,),
        in_specs=[
            whole_block(depth_table.shape),
            whole_block(row_table.shape),
            pl.BlockSpec(memory_space=pltpu.SMEM),
            pl.BlockSpec((1, rows, depth), lambda i: (t, 0, 0)),
            pl.BlockSpec((1, rows, depth), lambda i: (t, 0, 0)),
            pl.BlockSpec(
                (some, block_rows, depth),
                lambda i: (jnp.minimum(i, spreads - 1), unit // units, 0),
            ),
            pl.BlockSpec((coils, step, 2 * rows, depth), lambda i: (0, from_whole(i), 0, 0)),
            pl.BlockSpec((coils, step, 2, rows, depth), lambda i: (0, from_whole(i), 0, 0, 0)),
            pl.BlockSpec((step, 2, rows, depth), lambda i: (from_whole(i), 0, 0, 0)),
        ],
        out_specs=pl.BlockSpec((step, 2, rows, depth), lambda i: (plane(i), 0, 0, 0)),
        out_shape=jax.ShapeDtypeStruct((planes, 2, rows, depth), BF16),
        scratch_shapes=[
            pltpu.VMEM((rows * coils * width, depth), F32),
            pltpu.VMEM((2, coils, full + shared, width, depth), F32),
        ],
        compiler_params=params(),
        cost_estimate=cost(3e9, 10e6),
        name="back",
    )(depth_table, row_table, base[t, 0], place, mask, data, lines, maps, phase)


def gradient_kernel(points, block, mix_ref, *rest):
    own_refs, far_refs, out_ref = rest[:points], rest[points : 2 * points], rest[-1]
    ranks, planes, rows2, depth = out_ref.shape
    @pl.loop(0, planes, unroll=math.gcd(planes, BACK_UNROLL))
    def one(x):
        for i in range(rows2 // (2 * block)):
            at = slice(i * block, (i + 1) * block)
            columns = [
                jnp.concatenate(
                    [refs[t][x, p, at, :] for t in range(points) for p in range(2)], axis=0
                )
                for refs in (own_refs, far_refs)
            ]
            both = jnp.dot(
                mix_ref[...], jnp.concatenate(columns, axis=1), preferred_element_type=F32
            )
            total = both[:, :depth] + both[:, depth:]
            out_ref[:, x, 2 * i * block : 2 * (i + 1) * block, :] = total.reshape(
                ranks, 2 * block, depth
            )


def gradient(mix, own, far, ranks, slab, start, planes, before):
    points = len(own)
    _, _, rows, depth = own[0].shape
    step = math.gcd(planes, GRADIENT_PLANES)

    def block(part):
        first = start // step if part.shape[0] == slab else 0
        return pl.BlockSpec((step, 2, rows, depth), lambda x: (first + x, 0, 0, 0))

    parts = [*own, *far]
    more = [] if before is None else [before]
    return pl.pallas_call(
        functools.partial(gradient_kernel, points, mix.shape[1] // (2 * points)),
        grid=(planes // step,),
        in_specs=[whole_block(mix.shape)]
        + [block(part) for part in parts]
        + [pl.BlockSpec(memory_space=pl.ANY)] * len(more),
        out_specs=pl.BlockSpec(
            (ranks, step, 2 * rows, depth), lambda x: (0, start // step + x, 0, 0)
        ),
        out_shape=jax.ShapeDtypeStruct((ranks, slab, 2 * rows, depth), F32),
        input_output_aliases={1 + len(parts): 0} if more else {},
        compiler_params=params(),
        cost_estimate=cost(4e9, 12e6),
        name="gradient",
    )(mix, *parts, *more)


def from_other_groups(part, axis):
    groups = lax.axis_size(axis)
    moved = [
        lax.ppermute(part, axis, [(g, (g + shift) % groups) for g in range(groups)])
        for shift in range(1, groups)
    ]
    if groups == 1:
        return jnp.zeros_like(part)
    if groups == 2:
        return moved[0]
    return sum(m.astype(F32) for m in moved).astype(BF16)


def shards(spatial_coef, temporal_basis, coil_maps, field_steps, kspace_data, sample_mask):
    points = temporal_basis.shape[2]
    ranks, slab, rows, _, depth = spatial_coef.shape
    coils = coil_maps.shape[0]
    first, slab_rows = kspace_data.shape[2:4]
    dests = lax.axis_size("space")
    basis = lax.dynamic_slice_in_dim(
        temporal_basis, lax.axis_index("coil") * ranks, ranks, axis=1
    )
    mix, adjoint = mix_factors(basis, 16, False), mix_factors(basis, 32, True)
    data = kspace_data.reshape(coils, points, first, 2 * slab_rows, depth)
    maps = coil_maps.reshape(coils, slab, 2 * rows, depth)
    coef = spatial_coef.reshape(ranks, slab, 2 * rows, depth)
    cells = slab_rows * depth
    half_tiles = -(-SENT_SIXTEENTHS * cells // (8 * depth))
    if coils % 2:
        half_tiles += half_tiles % 2
    fit = (half_tiles // 2, half_tiles % 2)
    slots = half_tiles * depth // 2
    width = 2 * first // dests
    mask_here = sample_mask.astype(BF16)
    held = -(-points * slab_rows // width)
    extra = jnp.pad(
        mask_here.reshape(points * slab_rows, depth),
        ((0, held * width - points * slab_rows), (0, 0)),
    ).reshape(held, width, depth)
    first_table = real_table(first, 1.0, out_interleaved=True)
    depth_forward, depth_back = real_table(depth, -1.0).T, real_table(depth, 1.0).T
    rows_forward, rows_back = real_table(rows, -1.0), real_table(rows, 1.0)

    def prepare(data, start, count, split=False):
        return transform_data(
            first_table, mask_here, extra, data, start, count, dests, fit, split
        )

    def send(sent):
        return lax.all_to_all(sent, "space", split_axis=0, concat_axis=0, tiled=True)

    def back(piece, arrived, lines):
        t, chunk, unit, start, planes_here = piece
        own = back_images(
            depth_back, rows_back, ranked, arrived[chunk], lines[t], planes, phases[t], t,
            (unit, start, planes_here), fit,
        )
        return own, from_other_groups(own, "coil")

    units = coils * fit[0] + (coils // 2) * fit[1]
    head = min(HEAD, points)
    split = points > head and coils % 4 == 0 and slab % 8 == 0
    pieces = [(t, 0, t * units, 0, slab) for t in range(head)]
    pieces += [(t, 1, (t - head) * units, 0, slab) for t in range(head, points)]
    if split:
        last = (points - 1 - head) * units
        pieces[-1] = (points - 1, 1, last, 0, slab // 2)
        pieces.append((points - 1, 2, 0, slab // 2, slab // 2))

    sent = prepare(data, 0, head)
    arrived = [send(sent[0])]
    coef, _ = lax.optimization_barrier((coef, sent[0]))
    turned, phases, planes = make_images(mix, coef, field_steps, maps, points)
    others = [from_other_groups(part, "coil") for part in turned]
    lines = [
        forward_lines(depth_forward, rows_forward, turned[t], others[t], planes)
        for t in range(points)
    ]
    if points > head:
        data, _ = lax.optimization_barrier((data, planes))
        sent = prepare(data, head, points - head, split)
        sent, _ = lax.optimization_barrier((sent, lines[: points - 1]))
        arrived.append(send(sent[0]))
    mask_all = arrived[0][:, head * units * width :].reshape(dests, held * width, depth)
    mask_all = mask_all[:, : points * slab_rows].reshape(dests, points, slab_rows, depth)
    ranked = rank_cells(mask_all, slots)
    early = [back(piece, arrived, lines) for piece in pieces if piece[1] == 0]

    def finish(early, lines, arrived, sent):
        arrived = arrived + [send(part) for part in sent[1:]]
        done = list(early)
        for piece in pieces[len(early) :]:
            behind = list(lines)
            behind[piece[0]], _ = lax.optimization_barrier((lines[piece[0]], done[-1][0]))
            done.append(back(piece, arrived, behind))
        own, far = zip(*done)
        out = None
        for i in range(points - 1, len(pieces)):
            whole = [*range(points - 1), i]
            out = gradient(
                adjoint, [own[k] for k in whole], [far[k] for k in whole], ranks, slab,
                *pieces[i][3:], out,
            )
        return out

    def finish_more(early, lines, arrived, sent):
        count = jnp.cumsum(mask_here.astype(F32).reshape(points, cells), axis=1)
        rest = jnp.where(count > slots, mask_here.reshape(points, cells), 0).astype(BF16)
        rest = rest.reshape(1, points, 1, slab_rows, 1, depth)
        table = real_table(first, 1.0).reshape(2, first, 2, first)
        moved = jnp.einsum(
            "ctxypz,qkpx->ctkqyz", kspace_data * rest, table, preferred_element_type=F32
        ).astype(BF16)
        moved = lax.all_to_all(moved, "space", split_axis=2, concat_axis=4, tiled=True)
        moved = moved.reshape(coils, points, slab, 2 * rows, depth)
        lines = [
            (lines[t].astype(F32) - moved[:, t].astype(F32)).astype(BF16) for t in range(points)
        ]
        early = [back(piece, arrived, lines) for piece in pieces[: len(early)]]
        return finish(early, lines, arrived, sent)

    most = jnp.max(jnp.sum(mask_all.astype(F32), axis=(2, 3)))
    result = lax.cond(most > slots, finish_more, finish, early, lines, arrived, sent)
    return result.reshape(ranks, slab, rows, 2, depth)


def solution(mesh):
    in_specs = (
        P("coil", "space", None, None, None),
        P(),
        P("coil", "space", None, None, None),
        P("space", None, None),
        P("coil", None, None, "space", None, None),
        P(None, "space", None),
    )
    out_specs = P("coil", "space", None, None, None)
    return jax.shard_map(shards, mesh=mesh, in_specs=in_specs, out_specs=out_specs, check_vma=False)
```
